32 devices in a mesh: groups: 2 (over y), expert: 4 (over x, core), tensor: 4 (over z).
Axes of the slice: x: 2, y: 2, z: 4, core: 2. Of those that a mesh axis runs over, the one named last changes fastest.
Arguments:
- tokens: bfloat16 [2, 8, 4096], P(None, 'groups', 'expert'), parts along dimension 1, may hold values from -6 to 6
- proj_gate: bfloat16 [4096, 8192], P('expert', 'tensor'), may hold values from -0.09375 to 0.09375
- proj_input: bfloat16 [4096, 8192], P('expert', 'tensor'), may hold values from -0.09375 to 0.09375
- proj_write: bfloat16 [4096, 1024], P('expert', 'tensor'), may hold values from -0.09375 to 0.09375
- proj_read: bfloat16 [4096, 1024], P('expert', 'tensor'), may hold values from -0.09375 to 0.09375
- proj_step: bfloat16 [4096, 128], P('expert', 'tensor'), may hold values from -0.09375 to 0.09375
- conv_input: float32 [4, 8192], P(None, 'tensor'), may hold values from -3 to 3
- conv_write: float32 [4, 1024], P(None, 'tensor'), may hold values from -3 to 3
- conv_read: float32 [4, 1024], P(None, 'tensor'), may hold values from -3 to 3
- window_input: bfloat16 [8, 3, 8192], P(('groups', 'expert'), None, 'tensor'), parts along dimension 0, may hold values from -6 to 6
- window_write: bfloat16 [8, 3, 1024], P(('groups', 'expert'), None, 'tensor'), parts along dimension 0, may hold values from -6 to 6
- window_read: bfloat16 [8, 3, 1024], P(('groups', 'expert'), None, 'tensor'), parts along dimension 0, may hold values from -6 to 6
- step_bias: float32 [128], P('tensor'), may hold values from -4.5 to -1.5
- decay_log: float32 [128], P('tensor'), may hold values from 0 to 2.7
- skip_gain: float32 [128], P('tensor'), may hold values from 0.5 to 1.5
- norm_gain: float32 [8192], P('tensor'), may hold values from 0.1 to 1.9
- ssm_state: float32 [8, 128, 64, 128], P(('groups', 'expert'), 'tensor'), parts along dimension 0, may hold values from -1.6 to 1.6
- out_proj: bfloat16 [8192, 4096], P('tensor', 'expert'), may hold values from -0.0625 to 0.0625
- expert_up: bfloat16 [16, 4096, 1024], P('expert', None, 'tensor'), may hold values from -0.09375 to 0.09375
- expert_down: bfloat16 [16, 1024, 4096], P('expert', 'tensor'), may hold values from -0.1875 to 0.1875
- expert_ids: int32 [2, 8, 8], P(None, 'groups'), parts along dimension 1, may hold values from 0 to 15, all different within a row; in each aligned block of 4 rows (0 to 3, 4 to 7, ..., all dimensions but the last counted through in order) at most 4 rows name the same one
- route_gates: float32 [2, 8, 8], P(None, 'groups'), parts along dimension 1, may hold values from 0.05 to 0.35
Outputs:
- mixed_out: bfloat16 [2, 8, 4096], P(None, 'groups', 'expert'), parts along dimension 1
- ssm_final: float32 [8, 128, 64, 128], P(('groups', 'expert'), 'tensor'), parts along dimension 0
- input_final: bfloat16 [8, 3, 8192], P(('groups', 'expert'), None, 'tensor'), parts along dimension 0
- write_final: bfloat16 [8, 3, 1024], P(('groups', 'expert'), None, 'tensor'), parts along dimension 0
- read_final: bfloat16 [8, 3, 1024], P(('groups', 'expert'), None, 'tensor'), parts along dimension 0
The draws below stay inside these ranges and needn't reach their ends.
There are 2 independent parts, one for each index of `groups`. The reference program is written for one: setup_inputs(seed, part) draws one part's arguments, and reference() takes and returns one part's arrays. A program takes and returns all parts, laid end to end along the dimension named above; an argument that names none is the same for every part. Nothing has to cross between parts.
Inputs may be any that keep to these rules, and one draw needn't show every extreme that they name: `expert_ids`: each row names 8 different experts. In each step no expert is named by more than 4 rows, and in some step some expert is named by exactly 4 rows.
All inputs are finite; a program needn't handle non-finite values.
Results may differ from the reference program's by a relative error of at most 0.0066.
Values may be sent and summed in bfloat16 or wider, within the bound.
No kernel may reach another device: no remote copies, remote signals or barrier semaphores. Data moves between devices by JAX's collectives and lax.ppermute only.
A program may use at most 128 MiB of HBM per device.

```python
import math
import jax
import jax.numpy as jnp
import numpy as np
from jax import lax

D = 4096
HEADS = 128
HEAD_DIM = 64
STATE = 128
NGROUPS = 8
CONV = 4
EXPERT_HIDDEN = 1024
TOPK = 8
STEPS = 2
ROWS = 4
EXPERTS = 16
CAP = 4
INNER = 8192
BC = 1024


def level_of(key, extent, cuts, smallest, high):
    factor_of, own = 1.0, jax.random.fold_in(key, 6)
    for position, shards_of in cuts:
        steps = jnp.exp(jax.random.uniform(jax.random.fold_in(own, position), (shards_of,), jnp.float32, smallest / len(cuts), high / len(cuts)))
        factor_of = factor_of * jnp.repeat(steps, extent[position] // shards_of).reshape([-1 if axis == position else 1 for axis in range(len(extent))])
    return factor_of


def shared_out(stream_key, own, number, rows, count, top, limit, lean):
    order = jax.random.permutation(stream_key, count)
    heavy_load, ordinary = shares(count, rows * top, limit, lean, True), shares(count, rows * top, limit, lean, False)
    places = jnp.arange(count)

    def named(sizes, turn):
        used = int((sizes > 0).sum())
        fixed = max(1, used // 4)
        moved = fixed + (places - fixed + turn * (used - fixed)) % max(1, count - fixed)
        return jnp.zeros((count,), jnp.int32).at[order[jnp.where(places < fixed, places, moved)]].set(jnp.asarray(sizes, jnp.int32))

    sizes = jnp.where(number % 4 == 0, named(heavy_load, number // 4), named(ordinary, number - number // 4 - 1))
    mixed = jax.random.permutation(jax.random.fold_in(own, 3), count)
    giver, sink = mixed[0:count // 2 * 2:2], mixed[1:count // 2 * 2:2]
    slack = jnp.minimum(sizes[giver] - 1, limit - sizes[sink]) // 2
    slack = jnp.where((giver == order[0]) | (sink == order[0]) | (sizes[sink] == 0), 0, jnp.maximum(slack, 0))
    moved = jax.random.randint(jax.random.fold_in(own, 4), (count // 2,), 0, 1 << 20) % (slack + 1)
    sizes = sizes.at[giver].add(-moved).at[sink].add(moved)
    items = jnp.searchsorted(jnp.cumsum(sizes), jnp.arange(rows * top), side="right").astype(jnp.int32)
    grid = items.reshape(top, rows).T
    grid = grid[jax.random.permutation(jax.random.fold_in(own, 1), rows)]
    turn = jax.random.randint(jax.random.fold_in(own, 2), (rows, 1), 0, top)
    return jnp.take_along_axis(grid, (jnp.arange(top)[None, :] + turn) % top, axis=1)


def shares(amount, total, most, skew, full):
    weights = [(1 << 20) // math.isqrt(rank ** skew) + 1 for rank in range(1, amount + 1)]
    largest = most if full else min(most, max(-(-total // amount), total * weights[0] // sum(weights)))
    least = 1 if total - largest >= amount - 1 else 0
    counts, spare = [largest] + [least] * (amount - 1), total - largest - least * (amount - 1)
    while spare > 0:
        candidates = [i for i in range(1, amount) if counts[i] < largest] or [i for i in range(1, amount) if counts[i] < most]
        mass, remaining = sum([weights[i] for i in candidates]), spare
        for i in candidates:
            extra = min(most - counts[i], max(1, remaining * weights[i] // mass), spare)
            counts[i] = counts[i] + extra
            spare = spare - extra
    return np.array(counts)


def normal_values(stream_key, dims, deviation, bound, shards=(), kind=jnp.bfloat16):
    array = jax.random.normal(stream_key, dims, jnp.float32) * deviation
    if len(shards) > 0:
        array = level_of(stream_key, dims, shards, -0.22, 0.18) * array
    return jnp.clip(array, min=-bound, max=bound).astype(kind)


def setup_inputs(seed: int = 0, part: int = 0) -> dict:
    seeds = jax.random.split(jax.random.key(seed), 23)
    part_splits = jax.random.split(jax.random.fold_in(seeds[22], part), 23)
    tokens = normal_values(part_splits[0], (STEPS, ROWS, D), 1.0, 6.0, ((2, 4),))
    proj_gate = normal_values(seeds[1], (D, INNER), D ** -0.5, 0.09375, ((0, 4), (1, 4)))
    proj_input = normal_values(seeds[2], (D, INNER), D ** -0.5, 0.09375, ((0, 4), (1, 4)))
    proj_write = normal_values(seeds[3], (D, BC), D ** -0.5, 0.09375, ((0, 4), (1, 4)))
    proj_read = normal_values(seeds[4], (D, BC), D ** -0.5, 0.09375, ((0, 4), (1, 4)))
    proj_step = normal_values(seeds[5], (D, HEADS), D ** -0.5, 0.09375, ((0, 4), (1, 4)))
    conv_input = normal_values(seeds[6], (CONV, INNER), CONV ** -0.5, 3.0, ((1, 4),), jnp.float32)
    conv_write = normal_values(seeds[7], (CONV, BC), CONV ** -0.5, 3.0, ((1, 4),), jnp.float32)
    conv_read = normal_values(seeds[8], (CONV, BC), CONV ** -0.5, 3.0, ((1, 4),), jnp.float32)
    window_input = normal_values(part_splits[9], (ROWS, CONV - 1, INNER), 1.0, 6.0, ((0, 4), (2, 4)))
    window_write = normal_values(part_splits[10], (ROWS, CONV - 1, BC), 1.0, 6.0, ((0, 4), (2, 4)))
    window_read = normal_values(part_splits[11], (ROWS, CONV - 1, BC), 1.0, 6.0, ((0, 4), (2, 4)))
    step_bias = jnp.clip(-4.5 + 3.0 * jax.random.uniform(seeds[12], (HEADS,), jnp.float32) ** level_of(seeds[12], (HEADS,), ((0, 4),), -0.2, 0.2), -4.5, -1.5)
    decay_log = jnp.clip(2.7 * jax.random.uniform(seeds[13], (HEADS,), jnp.float32) ** level_of(seeds[13], (HEADS,), ((0, 4),), -0.2, 0.2), 0.0, 2.7)
    skip_gain = jnp.clip(0.5 + 1.0 * jax.random.uniform(seeds[14], (HEADS,), jnp.float32) ** level_of(seeds[14], (HEADS,), ((0, 4),), -0.2, 0.2), 0.5, 1.5)
    norm_gain = jnp.clip(1.0 + 0.18 * jax.random.normal(seeds[15], (INNER,), jnp.float32), 0.1, 1.9)
    ssm_state = normal_values(part_splits[16], (ROWS, HEADS, HEAD_DIM, STATE), 0.2, 1.6, ((0, 4), (1, 4)), jnp.float32)
    out_proj = normal_values(seeds[17], (INNER, D), INNER ** -0.5, 0.0625, ((0, 4), (1, 4)))
    expert_up = normal_values(seeds[18], (EXPERTS, D, EXPERT_HIDDEN), D ** -0.5, 0.09375, ((0, 4), (2, 4)))
    expert_down = normal_values(seeds[19], (EXPERTS, EXPERT_HIDDEN, D), EXPERT_HIDDEN ** -0.5, 0.1875, ((0, 4), (1, 4)))
    expert_ids_keys = jax.random.split(jax.random.fold_in(part_splits[20], 1), STEPS * ROWS // ROWS)
    expert_ids_turns = jax.random.permutation(jax.random.fold_in(part_splits[20], 3), STEPS * ROWS // ROWS)
    expert_ids = jax.vmap(lambda own, number: shared_out(jax.random.fold_in(part_splits[20], 2), own, number, ROWS, EXPERTS, TOPK, CAP, 2))(expert_ids_keys, expert_ids_turns).reshape((STEPS, ROWS, TOPK))
    route_gates = jnp.clip(jax.random.uniform(part_splits[21], (STEPS, ROWS, TOPK), jnp.float32, 0.05, 0.35), 0.05, 0.35)
    return {"tokens": tokens, "proj_gate": proj_gate, "proj_input": proj_input, "proj_write": proj_write, "proj_read": proj_read, "proj_step": proj_step, "conv_input": conv_input, "conv_write": conv_write, "conv_read": conv_read, "window_input": window_input, "window_write": window_write, "window_read": window_read, "step_bias": step_bias, "decay_log": decay_log, "skip_gain": skip_gain, "norm_gain": norm_gain, "ssm_state": ssm_state, "out_proj": out_proj, "expert_up": expert_up, "expert_down": expert_down, "expert_ids": expert_ids, "route_gates": route_gates}


def silu_float(values):
    return values / (1.0 + jnp.exp(-values))

def convolve(window_state, newest, kernel):
    window = jnp.concatenate([window_state, newest[:, None, :]], axis=1)
    summed = lax.optimization_barrier(jnp.sum(window.astype(jnp.float32) * kernel[None, :, :], axis=1))
    return (silu_float(summed), window[:, 1:, :])

def reference(tokens, proj_gate, proj_input, proj_write, proj_read, proj_step, conv_input, conv_write, conv_read, window_input, window_write, window_read, step_bias, decay_log, skip_gain, norm_gain, ssm_state, out_proj, expert_up, expert_down, expert_ids, route_gates):
    heads_group = HEADS // NGROUPS
    ssm_now = ssm_state
    results = []
    for step_index in range(STEPS):
        current = tokens[step_index]
        gate_pre = jnp.dot(current, proj_gate, preferred_element_type=jnp.float32).astype(jnp.bfloat16)
        input_pre = jnp.dot(current, proj_input, preferred_element_type=jnp.float32).astype(jnp.bfloat16)
        write_pre = jnp.dot(current, proj_write, preferred_element_type=jnp.float32).astype(jnp.bfloat16)
        read_pre = jnp.dot(current, proj_read, preferred_element_type=jnp.float32).astype(jnp.bfloat16)
        step_pre = jnp.dot(current, proj_step, preferred_element_type=jnp.float32).astype(jnp.bfloat16)
        input_act, window_input = convolve(window_input, input_pre, conv_input)
        write_act, window_write = convolve(window_write, write_pre, conv_write)
        read_act, window_read = convolve(window_read, read_pre, conv_read)
        step_size = jax.nn.softplus(step_pre.astype(jnp.float32) + step_bias[None, :])
        decay_rate = jnp.exp(-step_size * jnp.exp(decay_log)[None, :])
        heads_input = input_act.reshape(ROWS, NGROUPS, heads_group, HEAD_DIM)
        write_grouped = write_act.reshape(ROWS, NGROUPS, 1, 1, STATE)
        read_grouped = read_act.reshape(ROWS, NGROUPS, 1, 1, STATE)
        grouped = ssm_now.reshape(ROWS, NGROUPS, heads_group, HEAD_DIM, STATE)
        grouped = decay_rate.reshape(ROWS, NGROUPS, heads_group, 1, 1) * grouped + step_size.reshape(ROWS, NGROUPS, heads_group, 1, 1) * heads_input[..., None] * write_grouped
        ssm_read = lax.optimization_barrier(jnp.sum(grouped * read_grouped, axis=-1)) + skip_gain.reshape(NGROUPS, heads_group, 1) * heads_input
        ssm_now = grouped.reshape(ROWS, HEADS, HEAD_DIM, STATE)
        gated_out = ssm_read.reshape(ROWS, NGROUPS, heads_group * HEAD_DIM) * silu_float(gate_pre.astype(jnp.float32)).reshape(ROWS, NGROUPS, heads_group * HEAD_DIM)
        normed = gated_out * lax.rsqrt(lax.optimization_barrier(jnp.mean(gated_out * gated_out, axis=-1, keepdims=True)) + 1e-05) * norm_gain.reshape(NGROUPS, heads_group * HEAD_DIM)
        normed = normed.reshape(ROWS, INNER).astype(jnp.bfloat16)
        residual = current.astype(jnp.float32) + jnp.dot(normed, out_proj, preferred_element_type=jnp.float32)
        moe_in = residual.astype(jnp.bfloat16)
        chosen = expert_ids[step_index]
        weights_now = route_gates[step_index]

        def expert_pass(running, packed):
            up_weight, down_weight, expert_index = packed
            hidden = jnp.maximum(jnp.dot(moe_in, up_weight, preferred_element_type=jnp.float32), 0.0)
            hidden = (hidden * hidden).astype(jnp.bfloat16)
            expert_out = jnp.dot(hidden, down_weight, preferred_element_type=jnp.float32)
            row_weight = lax.optimization_barrier(jnp.sum(jnp.where(chosen == expert_index, weights_now, 0.0), axis=1))
            return (running + row_weight[:, None] * expert_out, None)
        moe_sum, _ = lax.scan(expert_pass, jnp.zeros((ROWS, D), jnp.float32), (expert_up, expert_down, jnp.arange(EXPERTS, dtype=jnp.int32)))
        results.append((residual + moe_sum).astype(jnp.bfloat16))
    return (jnp.stack(results), ssm_now, window_input, window_write, window_read)
```

```python
import jax
import jax.numpy as jnp
from jax import lax
from jax.sharding import PartitionSpec as P


def silu_float(values):
    return values / (1.0 + jnp.exp(-values))


def pairwise(axis):
    size = lax.axis_size(axis)
    return size <= 4 and size & (size - 1) == 0


def swap(values, axis, distance):
    size = lax.axis_size(axis)
    return lax.ppermute(values, axis, [(i, i ^ distance) for i in range(size)])


def gather(values, axis):
    size = lax.axis_size(axis)
    if not pairwise(axis):
        return lax.all_gather(values, axis, axis=0)
    held = [values] + [swap(values, axis, d) for d in range(1, size)]
    me = lax.axis_index(axis)
    bit = 1
    while bit < size:
        flip = (me & bit) != 0
        held = [jnp.where(flip, held[i ^ bit], held[i]) for i in range(size)]
        bit *= 2
    return jnp.stack(held)


def scatter_sum(blocks, axis):
    size = lax.axis_size(axis)
    if not pairwise(axis):
        return lax.psum_scatter(blocks, axis, scatter_dimension=0, tiled=False)
    me = lax.axis_index(axis)
    total = lax.dynamic_index_in_dim(blocks, me, 0, keepdims=False)
    sent = [
        swap(lax.dynamic_index_in_dim(blocks, me ^ d, 0, keepdims=False), axis, d)
        for d in range(1, size)
    ]
    for part in sent:
        total = total + part
    return total


def sum_over(values, axis):
    if not pairwise(axis):
        return lax.psum(values, axis)
    sent = [swap(values, axis, d) for d in range(1, lax.axis_size(axis))]
    total = values
    for part in sent:
        total = total + part
    return total


def convolve(window_state, newest, kernel):
    taps = kernel.shape[0]
    steps = newest.shape[1]
    window = jnp.concatenate([window_state, newest], axis=1)
    wide = window.astype(jnp.float32)
    acts = []
    for s in range(steps):
        acts.append(silu_float(jnp.sum(wide[:, s : s + taps] * kernel[None], axis=1)))
    return acts, window[:, steps:]


def per_device(
    tokens,
    proj_gate,
    proj_input,
    proj_write,
    proj_read,
    proj_step,
    conv_input,
    conv_write,
    conv_read,
    window_input,
    window_write,
    window_read,
    step_bias,
    decay_log,
    skip_gain,
    norm_gain,
    ssm_state,
    out_proj,
    expert_up,
    expert_down,
    expert_ids,
    route_gates,
):
    steps, rows, features = tokens.shape
    owners = lax.axis_size("expert")
    own_rows, heads, head_dim, state_size = ssm_state.shape
    inner = conv_input.shape[1]
    write_width = conv_write.shape[1]
    groups = write_width // state_size
    heads_group = heads // groups
    local_experts = expert_up.shape[0]
    many = rows * steps

    current = tokens.transpose(1, 0, 2).reshape(many, features)
    projected = jnp.concatenate(
        [
            jnp.dot(current, w, preferred_element_type=jnp.float32)
            for w in (proj_gate, proj_input, proj_write, proj_read, proj_step)
        ],
        axis=1,
    )
    projected = scatter_sum(projected.reshape(owners, own_rows, steps, -1), "expert")
    projected = projected.astype(jnp.bfloat16)
    edges = (inner, 2 * inner, 2 * inner + write_width, 2 * inner + 2 * write_width)
    gate_pre, input_pre, write_pre, read_pre, step_pre = jnp.split(projected, edges, axis=2)
    input_acts, input_final = convolve(window_input, input_pre, conv_input)
    write_acts, write_final = convolve(window_write, write_pre, conv_write)
    read_acts, read_final = convolve(window_read, read_pre, conv_read)

    state = ssm_state.reshape(own_rows, groups, heads_group, head_dim, state_size)
    normed = []
    for s in range(steps):
        step_size = jax.nn.softplus(step_pre[:, s].astype(jnp.float32) + step_bias[None, :])
        decay_rate = jnp.exp(-step_size * jnp.exp(decay_log)[None, :])
        heads_input = input_acts[s].reshape(own_rows, groups, heads_group, head_dim)
        write_grouped = write_acts[s].reshape(own_rows, groups, 1, 1, state_size)
        read_grouped = read_acts[s].reshape(own_rows, groups, 1, 1, state_size)
        state = (
            decay_rate.reshape(own_rows, groups, heads_group, 1, 1) * state
            + step_size.reshape(own_rows, groups, heads_group, 1, 1)
            * heads_input[..., None]
            * write_grouped
        )
        ssm_read = (
            jnp.sum(state * read_grouped, axis=-1)
            + skip_gain.reshape(groups, heads_group, 1) * heads_input
        )
        gated = ssm_read.reshape(own_rows, groups, -1) * silu_float(
            gate_pre[:, s].astype(jnp.float32)
        ).reshape(own_rows, groups, -1)
        scaled = (
            gated
            * lax.rsqrt(jnp.mean(gated * gated, axis=-1, keepdims=True) + 1e-05)
            * norm_gain.reshape(groups, -1)
        )
        normed.append(scaled.reshape(own_rows, inner).astype(jnp.bfloat16))
    ssm_final = state.reshape(ssm_state.shape)

    normed = gather(jnp.stack(normed, axis=1), "expert").reshape(many, inner)
    partial = jnp.dot(normed, out_proj, preferred_element_type=jnp.float32)
    residual = current.astype(jnp.float32) + sum_over(partial, "tensor")
    moe_in = gather(residual.astype(jnp.bfloat16), "expert")
    moe_in = moe_in.transpose(1, 0, 2).reshape(many, owners * features)

    first = lax.axis_index("expert") * local_experts
    chosen = expert_ids.transpose(1, 0, 2).reshape(many, -1)
    weights = route_gates.transpose(1, 0, 2).reshape(many, -1)
    moe_sum = jnp.zeros((many, owners * features), jnp.float32)
    for e in range(local_experts):
        hidden = jnp.dot(moe_in, expert_up[e], preferred_element_type=jnp.float32)
        hidden = jnp.maximum(hidden, 0.0)
        hidden = (hidden * hidden).astype(jnp.bfloat16)
        expert_out = jnp.dot(hidden, expert_down[e], preferred_element_type=jnp.float32)
        row_weight = jnp.sum(jnp.where(chosen == first + e, weights, 0.0), axis=1)
        moe_sum = moe_sum + row_weight[:, None] * expert_out
    blocks = moe_sum.reshape(many, owners, features).transpose(1, 0, 2)
    moe_sum = sum_over(scatter_sum(blocks, "expert"), "tensor")
    mixed = (residual + moe_sum).astype(jnp.bfloat16)
    mixed_out = mixed.reshape(rows, steps, features).transpose(1, 0, 2)
    return (mixed_out, ssm_final, input_final, write_final, read_final)


def solution(mesh):
    placed = (
        P(None, "groups", "expert"),
        P("expert", "tensor"),
        P("expert", "tensor"),
        P("expert", "tensor"),
        P("expert", "tensor"),
        P("expert", "tensor"),
        P(None, "tensor"),
        P(None, "tensor"),
        P(None, "tensor"),
        P(("groups", "expert"), None, "tensor"),
        P(("groups", "expert"), None, "tensor"),
        P(("groups", "expert"), None, "tensor"),
        P("tensor"),
        P("tensor"),
        P("tensor"),
        P("tensor"),
        P(("groups", "expert"), "tensor", None, None),
        P("tensor", "expert"),
        P("expert", None, "tensor"),
        P("expert", "tensor", None),
        P(None, "groups", None),
        P(None, "groups", None),
    )
    return jax.shard_map(
        per_device,
        mesh=mesh,
        in_specs=placed,
        out_specs=(
            P(None, "groups", "expert"),
            P(("groups", "expert"), "tensor", None, None),
            P(("groups", "expert"), None, "tensor"),
            P(("groups", "expert"), None, "tensor"),
            P(("groups", "expert"), None, "tensor"),
        ),
        check_vma=False,
    )
```

```python
import jax
import jax.numpy as jnp
from jax import lax
from jax.experimental import pallas as pl
from jax.experimental.pallas import tpu as pltpu
from jax.sharding import PartitionSpec as P


def silu_float(values):
    return values / (1.0 + jnp.exp(-values))


def pairwise(axis):
    size = lax.axis_size(axis)
    return size <= 4 and size & (size - 1) == 0


def swap(values, axis, distance):
    size = lax.axis_size(axis)
    return lax.ppermute(values, axis, [(i, i ^ distance) for i in range(size)])


def gather(values, axis):
    size = lax.axis_size(axis)
    if not pairwise(axis):
        return lax.all_gather(values, axis, axis=0)
    held = [values] + [swap(values, axis, d) for d in range(1, size)]
    me = lax.axis_index(axis)
    bit = 1
    while bit < size:
        flip = (me & bit) != 0
        held = [jnp.where(flip, held[i ^ bit], held[i]) for i in range(size)]
        bit *= 2
    return jnp.stack(held)


def sum_over(values, axis):
    if not pairwise(axis):
        return lax.psum(values, axis)
    sent = [swap(values, axis, d) for d in range(1, lax.axis_size(axis))]
    total = values
    for part in sent:
        total = total + part
    return total


def scatter_sum(blocks, axis):
    if not pairwise(axis):
        return lax.psum_scatter(jnp.stack(blocks), axis, scatter_dimension=0, tiled=False)
    total = blocks[0]
    for part in [swap(blocks[d], axis, d) for d in range(1, len(blocks))]:
        total = total + part
    return total


def owner_of(slot, axis):
    return lax.axis_index(axis) ^ slot if pairwise(axis) else slot


VMEM_LIMIT = 20 * 1024 * 1024
IN_VMEM = pl.BlockSpec(memory_space=pltpu.VMEM)
IN_HBM = pl.BlockSpec(memory_space=pl.ANY)
CHUNK = 512


def project(owners, tokens, weights, step_weights):
    steps, rows, depth = tokens.shape
    own_rows = rows // owners
    widths = [w.shape[1] for w in weights]
    heads = step_weights.shape[0]
    columns = sum(widths) + heads
    block = own_rows * steps
    pieces = []
    base = 0
    for index, width in enumerate(widths):
        for start in range(0, width, CHUNK):
            size = min(CHUNK, width - start)
            pieces.append((index, start, base + start, size))
        base += width

    def body(*refs):
        tokens_ref, step_ref = refs[:2]
        weight_refs = refs[2 : 2 + len(weights)]
        outs = refs[2 + len(weights) : 2 + len(weights) + owners]
        held, wide, lhs, sems = refs[2 + len(weights) + owners :]
        copies = [
            pltpu.make_async_copy(
                weight_refs[index].at[:, pl.ds(start, size)],
                held.at[:, pl.ds(place, size)],
                sems.at[i],
            )
            for i, (index, start, place, size) in enumerate(pieces)
        ]
        for copy in copies:
            copy.start()
        wide[...] = tokens_ref[...].astype(jnp.float32)
        for slot in range(owners):
            owner = owner_of(slot, "expert")
            for own in range(own_rows):
                for s in range(steps):
                    row = slot * block + own * steps + s
                    lhs[pl.ds(row, 1), :] = wide[s, pl.ds(owner * own_rows + own, 1), :]
        rows_in = lhs[...].astype(jnp.bfloat16)

        def put(place, size, result):
            for slot in range(owners):
                outs[slot][:, pl.ds(place, size)] = result[slot * block : (slot + 1) * block]

        put(
            columns - heads,
            heads,
            lax.dot_general(
                rows_in,
                step_ref[...],
                (((1,), (1,)), ((), ())),
                preferred_element_type=jnp.float32,
            ),
        )
        for copy, (_, _, place, size) in zip(copies, pieces):
            copy.wait()
            put(
                place,
                size,
                jnp.dot(
                    rows_in, held[:, pl.ds(place, size)], preferred_element_type=jnp.float32
                ),
            )

    return pl.pallas_call(
        body,
        out_shape=[jax.ShapeDtypeStruct((block, columns), jnp.float32)] * owners,
        in_specs=[IN_VMEM, IN_VMEM] + [IN_HBM] * len(weights),
        out_specs=[IN_VMEM] * owners,
        scratch_shapes=[
            pltpu.VMEM((depth, sum(widths)), jnp.bfloat16),
            pltpu.VMEM((steps, rows, depth), jnp.float32),
            pltpu.VMEM((owners * block, depth), jnp.float32),
            pltpu.SemaphoreType.DMA((len(pieces),)),
        ],
        compiler_params=pltpu.CompilerParams(vmem_limit_bytes=VMEM_LIMIT),
        name="project",
    )(tokens, step_weights, *weights)


def times_resident(lhs, weights):
    def body(lhs_ref, weights_ref, out_ref):
        out_ref[...] = jnp.dot(lhs_ref[...], weights_ref[...], preferred_element_type=jnp.float32)

    return pl.pallas_call(
        body,
        out_shape=jax.ShapeDtypeStruct((lhs.shape[0], weights.shape[1]), jnp.float32),
        in_specs=[IN_VMEM, IN_VMEM],
        out_specs=IN_VMEM,
        compiler_params=pltpu.CompilerParams(vmem_limit_bytes=VMEM_LIMIT),
        name="out_projection",
    )(lhs, pltpu.with_memory_space_constraint(weights, pltpu.VMEM))


def experts(moe_in, chosen, gates, expert_up, expert_down):
    owners, many, width = moe_in.shape
    local_experts, _, hidden_width = expert_up.shape

    def body(in_ref, chosen_ref, gates_ref, up_ref, down_ref, *refs):
        outs, hidden_ref = refs[:-1], refs[-1]
        first = lax.axis_index("expert") * local_experts
        row_weights = []
        for e in range(local_experts):
            total = jnp.zeros((many, hidden_width), jnp.float32)
            for j in range(owners):
                total += jnp.dot(
                    in_ref[j],
                    up_ref[e, pl.ds(j * width, width), :],
                    preferred_element_type=jnp.float32,
                )
            total = jnp.maximum(total, 0.0)
            hidden_ref[e] = (total * total).astype(jnp.bfloat16)
            row_weights.append(
                jnp.sum(
                    jnp.where(chosen_ref[...] == first + e, gates_ref[...], 0.0),
                    axis=1,
                    keepdims=True,
                )
            )
        for slot in range(owners):
            start = owner_of(slot, "expert") * width
            if pairwise("expert"):
                start = pl.multiple_of(start, width)
            total = jnp.zeros((many, width), jnp.float32)
            for e in range(local_experts):
                total += row_weights[e] * jnp.dot(
                    hidden_ref[e],
                    down_ref[e, :, pl.ds(start, width)],
                    preferred_element_type=jnp.float32,
                )
            outs[slot][...] = total

    return pl.pallas_call(
        body,
        out_shape=[jax.ShapeDtypeStruct((many, width), jnp.float32)] * owners,
        in_specs=[IN_VMEM] * 5,
        out_specs=[IN_VMEM] * owners,
        scratch_shapes=[pltpu.VMEM((local_experts, many, hidden_width), jnp.bfloat16)],
        compiler_params=pltpu.CompilerParams(vmem_limit_bytes=VMEM_LIMIT),
        name="experts",
    )(
        moe_in,
        chosen,
        gates,
        pltpu.with_memory_space_constraint(expert_up, pltpu.VMEM),
        pltpu.with_memory_space_constraint(expert_down, pltpu.VMEM),
    )


def convolve(window_state, newest, kernel):
    taps = kernel.shape[0]
    steps = newest.shape[1]
    window = jnp.concatenate([window_state, newest], axis=1)
    wide = window.astype(jnp.float32)
    acts = []
    for s in range(steps):
        acts.append(silu_float(jnp.sum(wide[:, s : s + taps] * kernel[None], axis=1)))
    return acts, window[:, steps:]


def per_device(
    tokens,
    proj_gate,
    proj_input,
    proj_write,
    proj_read,
    proj_step,
    conv_input,
    conv_write,
    conv_read,
    window_input,
    window_write,
    window_read,
    step_bias,
    decay_log,
    skip_gain,
    norm_gain,
    ssm_state,
    out_proj,
    expert_up,
    expert_down,
    expert_ids,
    route_gates,
):
    steps, rows, features = tokens.shape
    owners = lax.axis_size("expert")
    own_rows, heads, head_dim, state_size = ssm_state.shape
    inner = conv_input.shape[1]
    write_width = conv_write.shape[1]
    groups = write_width // state_size
    heads_group = heads // groups
    many = rows * steps

    projected = project(
        owners, tokens, (proj_gate, proj_input, proj_write, proj_read), proj_step.T
    )
    projected = scatter_sum(projected, "expert").astype(jnp.bfloat16)
    projected = projected.reshape(own_rows, steps, -1)
    edges = (inner, 2 * inner, 2 * inner + write_width, 2 * inner + 2 * write_width)
    gate_pre, input_pre, write_pre, read_pre, step_pre = jnp.split(projected, edges, axis=2)
    input_acts, input_final = convolve(window_input, input_pre, conv_input)
    write_acts, write_final = convolve(window_write, write_pre, conv_write)
    read_acts, read_final = convolve(window_read, read_pre, conv_read)

    state = ssm_state.reshape(own_rows, groups, heads_group, head_dim, state_size)
    normed = []
    for s in range(steps):
        step_size = jax.nn.softplus(step_pre[:, s].astype(jnp.float32) + step_bias[None, :])
        decay_rate = jnp.exp(-step_size * jnp.exp(decay_log)[None, :])
        heads_input = input_acts[s].reshape(own_rows, groups, heads_group, head_dim)
        write_grouped = write_acts[s].reshape(own_rows, groups, 1, 1, state_size)
        read_grouped = read_acts[s].reshape(own_rows, groups, 1, 1, state_size)
        state = (
            decay_rate.reshape(own_rows, groups, heads_group, 1, 1) * state
            + step_size.reshape(own_rows, groups, heads_group, 1, 1)
            * heads_input[..., None]
            * write_grouped
        )
        ssm_read = (
            jnp.sum(state * read_grouped, axis=-1)
            + skip_gain.reshape(groups, heads_group, 1) * heads_input
        )
        gated = ssm_read.reshape(own_rows, groups, -1) * silu_float(
            gate_pre[:, s].astype(jnp.float32)
        ).reshape(own_rows, groups, -1)
        scaled = (
            gated
            * lax.rsqrt(jnp.mean(gated * gated, axis=-1, keepdims=True) + 1e-05)
            * norm_gain.reshape(groups, -1)
        )
        normed.append(scaled.reshape(own_rows, inner).astype(jnp.bfloat16))
    ssm_final = state.reshape(ssm_state.shape)

    normed = gather(jnp.stack(normed), "expert")
    normed = normed.transpose(1, 0, 2, 3).reshape(many, inner)
    partial = times_resident(normed, out_proj)
    current = tokens.reshape(many, features).astype(jnp.float32)
    residual = current + sum_over(partial, "tensor")
    moe_in = gather(residual.astype(jnp.bfloat16), "expert")
    moe_sum = experts(
        moe_in,
        expert_ids.reshape(many, -1),
        route_gates.reshape(many, -1),
        expert_up,
        expert_down,
    )
    moe_sum = sum_over(scatter_sum(moe_sum, "expert"), "tensor")
    mixed_out = (residual + moe_sum).astype(jnp.bfloat16).reshape(tokens.shape)
    return (mixed_out, ssm_final, input_final, write_final, read_final)


def solution(mesh):
    placed = (
        P(None, "groups", "expert"),
        P("expert", "tensor"),
        P("expert", "tensor"),
        P("expert", "tensor"),
        P("expert", "tensor"),
        P("expert", "tensor"),
        P(None, "tensor"),
        P(None, "tensor"),
        P(None, "tensor"),
        P(("groups", "expert"), None, "tensor"),
        P(("groups", "expert"), None, "tensor"),
        P(("groups", "expert"), None, "tensor"),
        P("tensor"),
        P("tensor"),
        P("tensor"),
        P("tensor"),
        P(("groups", "expert"), "tensor", None, None),
        P("tensor", "expert"),
        P("expert", None, "tensor"),
        P("expert", "tensor", None),
        P(None, "groups", None),
        P(None, "groups", None),
    )
    return jax.shard_map(
        per_device,
        mesh=mesh,
        in_specs=placed,
        out_specs=(
            P(None, "groups", "expert"),
            P(("groups", "expert"), "tensor", None, None),
            P(("groups", "expert"), None, "tensor"),
            P(("groups", "expert"), None, "tensor"),
            P(("groups", "expert"), None, "tensor"),
        ),
        check_vma=False,
    )
```

```python
import jax
import jax.numpy as jnp
from jax import lax
from jax.experimental import pallas as pl
from jax.experimental.pallas import tpu as pltpu
from jax.sharding import PartitionSpec as P


def silu_float(values):
    return values / (1.0 + jnp.exp(-values))


def pairwise(axis):
    size = lax.axis_size(axis)
    return size <= 4 and size & (size - 1) == 0


def swap(values, axis, distance):
    size = lax.axis_size(axis)
    return lax.ppermute(values, axis, [(i, i ^ distance) for i in range(size)])


def gather(values, axis):
    size = lax.axis_size(axis)
    if not pairwise(axis):
        held = lax.all_gather(values, axis, axis=0)
        return [held[j] for j in range(size)]
    return [values] + [swap(values, axis, d) for d in range(1, size)]


def sum_parts(values, axis):
    return gather(values, axis) if pairwise(axis) else [lax.psum(values, axis)]


def scatter_parts(blocks, axis):
    if not pairwise(axis):
        return [lax.psum_scatter(jnp.stack(blocks), axis, scatter_dimension=0, tiled=False)]
    return [blocks[0]] + [swap(blocks[d], axis, d) for d in range(1, len(blocks))]


def added(parts):
    total = parts[0]
    for part in parts[1:]:
        total = total + part
    return total


def owner_of(slot, axis):
    return lax.axis_index(axis) ^ slot if pairwise(axis) else slot


VMEM_LIMIT = 16 * 1024 * 1024
IN_VMEM = pl.BlockSpec(memory_space=pltpu.VMEM)
IN_HBM = pl.BlockSpec(memory_space=pltpu.HBM)
CHUNK = 512


def local_kernel(body, name, out_shape, ins, scratch=(), bytes_accessed=1 << 20):
    return pl.pallas_call(
        body,
        out_shape=out_shape,
        in_specs=[spec for _, spec in ins],
        out_specs=jax.tree.map(lambda _: IN_VMEM, out_shape),
        scratch_shapes=list(scratch),
        compiler_params=pltpu.CompilerParams(vmem_limit_bytes=VMEM_LIMIT),
        cost_estimate=pl.CostEstimate(
            flops=bytes_accessed, bytes_accessed=bytes_accessed, transcendentals=0
        ),
        name=name,
    )(*[held(array, spec) for array, spec in ins])


def held(array, spec):
    if spec is IN_HBM:
        return pltpu.with_memory_space_constraint(array, pltpu.HBM)
    return array


def resident(array):
    return pltpu.with_memory_space_constraint(array, pltpu.VMEM)


def shaped(shape, dtype=jnp.float32):
    return jax.ShapeDtypeStruct(tuple(shape), dtype)


def project(owners, tokens, weights, step_weights):
    steps, rows, depth = tokens.shape
    own_rows = rows // owners
    widths = [w.shape[1] for w in weights]
    heads = step_weights.shape[0]
    columns = sum(widths) + heads
    block = own_rows * steps
    pieces = []
    base = 0
    for index, width in enumerate(widths):
        for start in range(0, width, CHUNK):
            size = min(CHUNK, width - start)
            pieces.append((index, start, base + start, size))
        base += width
    count = len(weights)

    def body(*refs):
        tokens_ref, step_ref = refs[:2]
        weight_refs = refs[2 : 2 + count]
        outs = refs[2 + count : 2 + count + owners]
        current_ref, tokens_in, step_in, weights_in, wide, lhs, sems = refs[2 + count + owners :]
        first = [
            pltpu.make_async_copy(tokens_ref, tokens_in, sems.at[0]),
            pltpu.make_async_copy(step_ref, step_in, sems.at[1]),
        ]
        copies = [
            pltpu.make_async_copy(
                weight_refs[index].at[:, pl.ds(start, size)],
                weights_in.at[:, pl.ds(place, size)],
                sems.at[2 + i],
            )
            for i, (index, start, place, size) in enumerate(pieces)
        ]
        for copy in first + copies:
            copy.start()
        first[0].wait()
        for s in range(steps):
            wide[s] = tokens_in[s].astype(jnp.float32)
            current_ref[pl.ds(s * rows, rows), :] = wide[s]
        for slot in range(owners):
            owner = owner_of(slot, "expert")
            for own in range(own_rows):
                for s in range(steps):
                    row = slot * block + own * steps + s
                    lhs[pl.ds(row, 1), :] = wide[s, pl.ds(owner * own_rows + own, 1), :]
        rows_in = lhs[...].astype(jnp.bfloat16)

        def put(place, size, result):
            for slot in range(owners):
                outs[slot][:, pl.ds(place, size)] = result[slot * block : (slot + 1) * block]

        first[1].wait()
        put(
            columns - heads,
            heads,
            lax.dot_general(
                rows_in,
                step_in[...],
                (((1,), (1,)), ((), ())),
                preferred_element_type=jnp.float32,
            ),
        )
        for copy, (_, _, place, size) in zip(copies, pieces):
            copy.wait()
            put(
                place,
                size,
                jnp.dot(
                    rows_in, weights_in[:, pl.ds(place, size)], preferred_element_type=jnp.float32
                ),
            )

    *blocks, current = local_kernel(
        body,
        "project",
        [shaped((block, columns))] * owners + [shaped((steps * rows, depth))],
        [(tokens, IN_HBM), (step_weights, IN_HBM)] + [(w, IN_HBM) for w in weights],
        [
            pltpu.VMEM(tokens.shape, jnp.bfloat16),
            pltpu.VMEM(step_weights.shape, jnp.bfloat16),
            pltpu.VMEM((depth, sum(widths)), jnp.bfloat16),
            pltpu.VMEM(tokens.shape, jnp.float32),
            pltpu.VMEM((owners * block, depth), jnp.float32),
            pltpu.SemaphoreType.DMA((2 + len(pieces),)),
        ],
        bytes_accessed=10 << 20,
    )
    return blocks, current


def split_in(values, terms):
    parts = []
    for _ in range(terms):
        part = values.astype(jnp.bfloat16)
        parts.append(part)
        values = values - part.astype(jnp.float32)
    return parts


def spread_heads(step_bias, decay_log, skip_gain, inner):
    heads = step_bias.shape[1]
    head_dim = inner // heads

    def body(bias_ref, decay_ref, skip_ref, params_ref, spread_ref):
        head = lax.broadcasted_iota(jnp.int32, (heads, inner), 0) * head_dim
        channel = lax.broadcasted_iota(jnp.int32, (heads, inner), 1)
        inside = (channel >= head) & (channel < head + head_dim)
        spread = jnp.where(inside, 1.0, 0.0).astype(jnp.bfloat16)
        spread_ref[...] = spread
        rows = jnp.concatenate([bias_ref[...], jnp.exp(decay_ref[...]), skip_ref[...]], axis=0)
        total = jnp.zeros((3, inner), jnp.float32)
        for part in reversed(split_in(rows, 3)):
            total += jnp.dot(part, spread, preferred_element_type=jnp.float32)
        params_ref[...] = total

    return local_kernel(
        body,
        "spread_heads",
        [shaped((3, inner)), shaped((heads, inner), jnp.bfloat16)],
        [(step_bias, IN_VMEM), (decay_log, IN_VMEM), (skip_gain, IN_VMEM)],
    )


def mix(parts, head_params, spread, convs, windows, norm_gain, ssm_state, steps):
    own_rows, heads, head_dim, state_size = ssm_state.shape
    block, columns = parts[0].shape
    inner, width = convs[0].shape[1], convs[1].shape[1]
    groups = width // state_size
    heads_group = heads // groups
    channels = heads_group * head_dim
    taps = convs[0].shape[0]
    count = len(parts)
    edges = (0, inner, 2 * inner, 2 * inner + width, 2 * inner + 2 * width, columns)
    terms = 1 + steps

    def body(*refs):
        part_refs = refs[:count]
        params_ref, spread_ref, *rest = refs[count:]
        conv_refs, window_refs = rest[:3], rest[3:6]
        gain_ref, state_ref, normed_ref, pre_ref, coef_ref, write_ref = rest[6:]
        total = part_refs[0][...]
        for ref in part_refs[1:]:
            total = total + ref[...]
        rounded = total.astype(jnp.bfloat16).astype(jnp.float32)
        pre_ref[...] = rounded[:, edges[1] : edges[4]]
        gate, *newest = [rounded[:, edges[i] : edges[i + 1]] for i in range(4)]
        bias, rate, skip = [params_ref[i : i + 1] for i in range(3)]
        step_pre = jnp.dot(
            rounded[:, edges[4] :].astype(jnp.bfloat16),
            spread_ref[...],
            preferred_element_type=jnp.float32,
        )
        step_size = jax.nn.softplus(step_pre + bias)
        decay = jnp.exp(-step_size * rate)
        gate = silu_float(gate)
        for own in range(own_rows):
            first = own * steps
            acts = []
            for which in range(3):
                taps_in = conv_refs[which][...]
                earlier = window_refs[which][own].astype(jnp.float32)
                line = [earlier[k : k + 1] for k in range(taps - 1)]
                line += [newest[which][first + s : first + s + 1] for s in range(steps)]
                acts.append(
                    [
                        silu_float(added([line[s + k] * taps_in[k : k + 1] for k in range(taps)]))
                        for s in range(steps)
                    ]
                )
            input_act, write_act, read_act = acts
            for s in range(steps):
                write_ref[pl.ds(first + s, 1), :] = write_act[s]
            sizes = [step_size[first + s : first + s + 1] for s in range(steps)]
            decays = [decay[first + s : first + s + 1] for s in range(steps)]
            fresh = [sizes[s] * input_act[s] for s in range(steps)]
            coefs = list(fresh)
            kept = jnp.ones_like(decays[0])
            for s in reversed(range(steps)):
                coefs[s] = coefs[s] * kept
                kept = kept * decays[s]
            for i, row in enumerate([kept] + coefs):
                coef_ref[own, i : i + 1, :] = row
            for g in range(groups):
                span = slice(g * channels, (g + 1) * channels)
                lanes = slice(g * state_size, (g + 1) * state_size)
                state = state_ref[own, g * heads_group : (g + 1) * heads_group]
                state = state.reshape(channels, state_size)
                reads = jnp.concatenate([read_act[s][:, lanes] for s in range(steps)], axis=0)
                high, low = [p.astype(jnp.float32) for p in split_in(reads, 2)]
                reads = jnp.concatenate([high, low], axis=0).astype(jnp.bfloat16)
                by_high, by_low = [
                    lax.dot_general(
                        reads, p, (((1,), (1,)), ((), ())), preferred_element_type=jnp.float32
                    )
                    for p in split_in(state, 2)
                ]
                product = by_high[:steps] + by_high[steps:] + by_low[:steps]
                for s in range(steps):
                    value = product[s : s + 1]
                    for j in range(s + 1):
                        overlap = jnp.sum(
                            write_act[j][:, lanes] * read_act[s][:, lanes], axis=1, keepdims=True
                        )
                        value = decays[j][:, span] * value + fresh[j][:, span] * overlap
                    value = value + skip[:, span] * input_act[s][:, span]
                    value = value * gate[first + s : first + s + 1, span]
                    mean = jnp.mean(value * value, axis=1, keepdims=True)
                    value = value * lax.rsqrt(mean + 1e-05) * gain_ref[:, span]
                    normed_ref[pl.ds(first + s, 1), span] = value.astype(jnp.bfloat16)

    return local_kernel(
        body,
        "mix",
        [
            shaped((block, inner), jnp.bfloat16),
            shaped((block, inner + 2 * width)),
            shaped((own_rows, terms, inner)),
            shaped((block, width)),
        ],
        [(a, IN_VMEM) for a in (*parts, head_params, spread, *convs, *windows, norm_gain, ssm_state)],
        bytes_accessed=4 << 20,
    )


def renew(pre, coefs, writes, windows, ssm_state, steps):
    own_rows, heads, head_dim, state_size = ssm_state.shape
    groups = writes.shape[1] // state_size
    heads_group = heads // groups
    inner = coefs.shape[2]
    widths = [w.shape[2] for w in windows]
    kept = windows[0].shape[1]

    def body(pre_ref, coef_ref, write_ref, *rest):
        window_refs, (state_ref, final_ref), out_refs = rest[:3], rest[3:5], rest[5:]
        for own in range(own_rows):
            first = own * steps
            base = 0
            for window_ref, out_ref, width in zip(window_refs, out_refs, widths):
                line = jnp.concatenate(
                    [
                        window_ref[own].astype(jnp.float32),
                        pre_ref[pl.ds(first, steps), pl.ds(base, width)],
                    ],
                    axis=0,
                )
                out_ref[own] = line[steps:].astype(jnp.bfloat16)
                base += width
            rows = jnp.concatenate(
                [coef_ref[own], jnp.zeros((8 - 1 - steps, inner), jnp.float32)], axis=0
            )
            for h in range(heads):
                lanes = slice((h // heads_group) * state_size, (h // heads_group + 1) * state_size)
                if h % 2 == 0:
                    pair = rows[:, h * head_dim : (h + 2) * head_dim].T
                columns = pair[(h % 2) * head_dim : (h % 2 + 1) * head_dim]
                value = columns[:, 0:1] * state_ref[own, h]
                for s in range(steps):
                    value = value + columns[:, 1 + s : 2 + s] * write_ref[pl.ds(first + s, 1), lanes]
                final_ref[own, h] = value

    return local_kernel(
        body,
        "renew",
        [shaped(ssm_state.shape)] + [shaped(w.shape, jnp.bfloat16) for w in windows],
        [(a, IN_VMEM) for a in (pre, coefs, writes, *windows, ssm_state)],
        bytes_accessed=2 << 20,
    )


def project_out(normed, out_proj, steps):
    owners = len(normed)
    block, inner = normed[0].shape
    own_rows = block // steps
    rows = own_rows * owners

    def body(*refs):
        weights_ref, out_ref, lhs = refs[owners:]
        for slot in range(owners):
            owner = owner_of(slot, "expert")
            values = refs[slot][...].astype(jnp.float32)
            for own in range(own_rows):
                for s in range(steps):
                    row = s * rows + owner * own_rows + own
                    lhs[pl.ds(row, 1), :] = values[own * steps + s : own * steps + s + 1]
        out_ref[...] = jnp.dot(
            lhs[...].astype(jnp.bfloat16), weights_ref[...], preferred_element_type=jnp.float32
        )

    return local_kernel(
        body,
        "project_out",
        shaped((rows * steps, out_proj.shape[1])),
        [(a, IN_VMEM) for a in (*normed, resident(out_proj))],
        [pltpu.VMEM((rows * steps, inner), jnp.float32)],
        bytes_accessed=4 << 20,
    )


def experts(moe_in, chosen, gates, expert_up, expert_down):
    owners = len(moe_in)
    many, width = moe_in[0].shape
    steps, rows, _ = chosen.shape
    local_experts, _, hidden_width = expert_up.shape

    def body(*refs):
        chosen_ref, gates_ref, up_ref, down_ref = refs[owners : owners + 4]
        outs, hidden_ref = refs[owners + 4 : -1], refs[-1]
        first = lax.axis_index("expert") * local_experts

        def span(slot):
            start = owner_of(slot, "expert") * width
            return pl.ds(pl.multiple_of(start, width) if pairwise("expert") else start, width)

        row_weights = []
        for e in range(local_experts):
            total = jnp.zeros((many, hidden_width), jnp.float32)
            for slot in range(owners):
                total += jnp.dot(
                    refs[slot][...], up_ref[e, span(slot), :], preferred_element_type=jnp.float32
                )
            total = jnp.maximum(total, 0.0)
            hidden_ref[e] = (total * total).astype(jnp.bfloat16)
            row_weights.append(
                jnp.concatenate(
                    [
                        jnp.sum(
                            jnp.where(chosen_ref[s] == first + e, gates_ref[s], 0.0),
                            axis=1,
                            keepdims=True,
                        )
                        for s in range(steps)
                    ],
                    axis=0,
                )
            )
        for slot in range(owners):
            total = jnp.zeros((many, width), jnp.float32)
            for e in range(local_experts):
                total += row_weights[e] * jnp.dot(
                    hidden_ref[e], down_ref[e, :, span(slot)], preferred_element_type=jnp.float32
                )
            outs[slot][...] = total

    return local_kernel(
        body,
        "experts",
        [shaped((many, width))] * owners,
        [
            (a, IN_VMEM)
            for a in (*moe_in, chosen, gates, resident(expert_up), resident(expert_down))
        ],
        [pltpu.VMEM((local_experts, many, hidden_width), jnp.bfloat16)],
        bytes_accessed=16 << 20,
    )


def finish(parts, shape):
    steps, rows, _ = shape

    def body(*refs):
        total = added([ref[...] for ref in refs[:-1]])
        for s in range(steps):
            refs[-1][s] = total[s * rows : (s + 1) * rows].astype(jnp.bfloat16)

    return local_kernel(body, "finish", shaped(shape, jnp.bfloat16), [(p, IN_VMEM) for p in parts])


def per_device(
    tokens,
    proj_gate,
    proj_input,
    proj_write,
    proj_read,
    proj_step,
    conv_input,
    conv_write,
    conv_read,
    window_input,
    window_write,
    window_read,
    step_bias,
    decay_log,
    skip_gain,
    norm_gain,
    ssm_state,
    out_proj,
    expert_up,
    expert_down,
    expert_ids,
    route_gates,
):
    steps = tokens.shape[0]
    inner = conv_input.shape[1]
    convs = (conv_input, conv_write, conv_read)
    windows = (window_input, window_write, window_read)
    head_params, spread = spread_heads(
        *[p.reshape(1, -1) for p in (step_bias, decay_log, skip_gain)], inner
    )
    projected, current = project(
        lax.axis_size("expert"),
        tokens,
        (proj_gate, proj_input, proj_write, proj_read),
        proj_step.T,
    )
    normed, pre, coefs, writes = mix(
        scatter_parts(projected, "expert"),
        head_params,
        spread,
        convs,
        windows,
        norm_gain.reshape(1, -1),
        ssm_state,
        steps,
    )
    partial = project_out(gather(normed, "expert"), out_proj, steps)
    ssm_final, *finals = renew(pre, coefs, writes, windows, ssm_state, steps)
    residual = added([current] + sum_parts(partial, "tensor"))
    moe_in = gather(residual.astype(jnp.bfloat16), "expert")
    moe_sum = experts(moe_in, expert_ids, route_gates, expert_up, expert_down)
    moe_sum = added(scatter_parts(moe_sum, "expert"))
    mixed_out = finish([residual] + sum_parts(moe_sum, "tensor"), tokens.shape)
    return (mixed_out, ssm_final, *finals)


def solution(mesh):
    placed = (
        P(None, "groups", "expert"),
        P("expert", "tensor"),
        P("expert", "tensor"),
        P("expert", "tensor"),
        P("expert", "tensor"),
        P("expert", "tensor"),
        P(None, "tensor"),
        P(None, "tensor"),
        P(None, "tensor"),
        P(("groups", "expert"), None, "tensor"),
        P(("groups", "expert"), None, "tensor"),
        P(("groups", "expert"), None, "tensor"),
        P("tensor"),
        P("tensor"),
        P("tensor"),
        P("tensor"),
        P(("groups", "expert"), "tensor", None, None),
        P("tensor", "expert"),
        P("expert", None, "tensor"),
        P("expert", "tensor", None),
        P(None, "groups", None),
        P(None, "groups", None),
    )
    return jax.shard_map(
        per_device,
        mesh=mesh,
        in_specs=placed,
        out_specs=(
            P(None, "groups", "expert"),
            P(("groups", "expert"), "tensor", None, None),
            P(("groups", "expert"), None, "tensor"),
            P(("groups", "expert"), None, "tensor"),
            P(("groups", "expert"), None, "tensor"),
        ),
        check_vma=False,
    )
```

```python
import jax
import jax.numpy as jnp
from jax import lax
from jax.experimental import pallas as pl
from jax.experimental.pallas import tpu as pltpu
from jax.sharding import PartitionSpec as P


def silu_float(values):
    return values / (1.0 + jnp.exp(-values))


def pairwise(axis):
    size = lax.axis_size(axis)
    return size <= 4 and size & (size - 1) == 0


def swap(values, axis, distance):
    size = lax.axis_size(axis)
    return lax.ppermute(values, axis, [(i, i ^ distance) for i in range(size)])


def gather(values, axis):
    size = lax.axis_size(axis)
    if not pairwise(axis):
        held = lax.all_gather(values, axis, axis=0)
        return [held[j] for j in range(size)]
    return [values] + [swap(values, axis, d) for d in range(1, size)]


def sum_parts(values, axis, sent=None):
    if not pairwise(axis):
        return [lax.psum(values, axis)]
    sent = values if sent is None else sent
    return [values] + [swap(sent, axis, d) for d in range(1, lax.axis_size(axis))]


def scatter_parts(blocks, axis):
    if not pairwise(axis):
        blocks = jnp.stack([block.astype(jnp.float32) for block in blocks])
        return [lax.psum_scatter(blocks, axis, scatter_dimension=0, tiled=False)]
    return [blocks[0]] + [swap(blocks[d], axis, d) for d in reversed(range(1, len(blocks)))]


def added(parts):
    total = parts[0]
    for part in parts[1:]:
        total = total + part.astype(total.dtype)
    return total


def owner_of(slot, axis):
    return lax.axis_index(axis) ^ slot if pairwise(axis) else slot


VMEM_LIMIT = 16 * 1024 * 1024
IN_VMEM = pl.BlockSpec(memory_space=pltpu.VMEM)
IN_HBM = pl.BlockSpec(memory_space=pltpu.HBM)
CHUNK = 512 * 1024
MIX_COST = 64 << 20


def local_kernel(body, name, out_shape, ins, scratch=(), bytes_accessed=1 << 20):
    return pl.pallas_call(
        body,
        out_shape=out_shape,
        in_specs=[spec for _, spec in ins],
        out_specs=jax.tree.map(lambda _: IN_VMEM, out_shape),
        scratch_shapes=list(scratch),
        compiler_params=pltpu.CompilerParams(vmem_limit_bytes=VMEM_LIMIT),
        cost_estimate=pl.CostEstimate(
            flops=bytes_accessed, bytes_accessed=bytes_accessed, transcendentals=0
        ),
        name=name,
    )(*[held(array, spec) for array, spec in ins])


def held(array, spec):
    if spec is IN_HBM:
        return pltpu.with_memory_space_constraint(array, pltpu.HBM)
    return array


def resident(array):
    return pltpu.with_memory_space_constraint(array, pltpu.VMEM)


def shaped(shape, dtype=jnp.float32):
    return jax.ShapeDtypeStruct(tuple(shape), dtype)


def sent_narrow(shape, slots):
    return [shaped(shape)] + [shaped(shape, jnp.bfloat16)] * (slots - 1)


def project(owners, tokens, weights, step_weights):
    steps, rows, depth = tokens.shape
    own_rows = rows // owners
    widths = [w.shape[1] for w in weights]
    heads = step_weights.shape[0]
    columns = sum(widths) + heads
    block = own_rows * steps
    pieces = []
    for index, width in enumerate(widths):
        size = max(16, min(depth, CHUNK // width))
        pieces += [(index, start, min(size, depth - start)) for start in range(0, depth, size)]
    bases = [sum(widths[:index]) for index in range(len(widths))]
    count = len(weights)

    def body(*refs):
        tokens_ref, step_ref = refs[:2]
        weight_refs = refs[2 : 2 + count]
        outs = refs[2 + count : 2 + count + owners]
        tokens_in, step_in, wide, lhs, sems, *weights_in = refs[2 + count + owners :]
        first = [
            pltpu.make_async_copy(tokens_ref, tokens_in, sems.at[0]),
            pltpu.make_async_copy(step_ref, step_in, sems.at[1]),
        ]
        copies = [
            pltpu.make_async_copy(
                weight_refs[index].at[pl.ds(start, size)],
                weights_in[index].at[pl.ds(start, size)],
                sems.at[2 + i],
            )
            for i, (index, start, size) in enumerate(pieces)
        ]
        for copy in first + copies:
            copy.start()
        first[0].wait()
        wide[...] = tokens_in[...].astype(jnp.float32)
        for slot in range(owners):
            owner = owner_of(slot, "expert")
            for own in range(own_rows):
                for s in range(steps):
                    row = slot * block + own * steps + s
                    lhs[pl.ds(row, 1), :] = wide[s, pl.ds(owner * own_rows + own, 1), :]
        rows_in = lhs[...].astype(jnp.bfloat16)

        def put(place, size, result):
            for slot in range(owners):
                part = result[slot * block : (slot + 1) * block]
                outs[slot][:, pl.ds(place, size)] = part.astype(outs[slot].dtype)

        first[1].wait()
        put(
            columns - heads,
            heads,
            lax.dot_general(
                rows_in,
                step_in[...],
                (((1,), (1,)), ((), ())),
                preferred_element_type=jnp.float32,
            ),
        )
        total = None
        for copy, (index, start, size) in zip(copies, pieces):
            copy.wait()
            product = jnp.dot(
                rows_in[:, start : start + size],
                weights_in[index][pl.ds(start, size)],
                preferred_element_type=jnp.float32,
            )
            total = product if start == 0 else total + product
            if start + size == depth:
                put(bases[index], widths[index], total)

    return local_kernel(
        body,
        "project",
        sent_narrow((block, columns), owners),
        [(tokens, IN_HBM), (step_weights, IN_HBM)] + [(w, IN_HBM) for w in weights],
        [
            pltpu.VMEM(tokens.shape, jnp.bfloat16),
            pltpu.VMEM(step_weights.shape, jnp.bfloat16),
            pltpu.VMEM(tokens.shape, jnp.float32),
            pltpu.VMEM((owners * block, depth), jnp.float32),
            pltpu.SemaphoreType.DMA((2 + len(pieces),)),
        ]
        + [pltpu.VMEM(w.shape, jnp.bfloat16) for w in weights],
        bytes_accessed=10 << 20,
    )


def split_in(values, terms):
    parts = []
    for _ in range(terms):
        part = values.astype(jnp.bfloat16)
        parts.append(part)
        values = values - part.astype(jnp.float32)
    return parts


def stacked(*parts):
    rows = sum(part.shape[0] for part in parts)
    parts = [part.astype(jnp.float32) for part in parts]
    parts.append(jnp.zeros((-rows % 8, parts[0].shape[1]), jnp.float32))
    return jnp.concatenate(parts, axis=0).astype(jnp.bfloat16)


def prepare(step_bias, decay_log, skip_gain, inner, arrays):
    heads = step_bias.shape[1]
    head_dim = inner // heads
    count = 3 + len(arrays)

    def body(*refs):
        sources, (params_ref, spread_ref), outs = refs[:count], refs[count : count + 2], refs[count + 2 :]
        loaded, sems = outs[:-2], outs[-1]
        rows_ref = outs[-2]
        targets = [rows_ref.at[pl.ds(i, 1)] for i in range(3)] + list(loaded)
        copies = [
            pltpu.make_async_copy(source, target, sems.at[i])
            for i, (source, target) in enumerate(zip(sources, targets))
        ]
        for copy in copies:
            copy.start()
        head = lax.broadcasted_iota(jnp.int32, (heads, inner), 0) * head_dim
        channel = lax.broadcasted_iota(jnp.int32, (heads, inner), 1)
        inside = (channel >= head) & (channel < head + head_dim)
        spread = jnp.where(inside, 1.0, 0.0).astype(jnp.bfloat16)
        spread_ref[...] = spread
        for copy in copies[:3]:
            copy.wait()
        rows = rows_ref[...]
        rows = jnp.concatenate([rows[0:1], jnp.exp(rows[1:2]), rows[2:3]], axis=0)
        total = jnp.zeros((3, inner), jnp.float32)
        for part in reversed(split_in(rows, 3)):
            total += jnp.dot(part, spread, preferred_element_type=jnp.float32)
        params_ref[...] = total
        for copy in copies[3:]:
            copy.wait()

    params, spread, *loaded = local_kernel(
        body,
        "prepare",
        [shaped((3, inner)), shaped((heads, inner), jnp.bfloat16)]
        + [shaped(a.shape, a.dtype) for a in arrays],
        [(a, IN_HBM) for a in (step_bias, decay_log, skip_gain, *arrays)],
        [pltpu.VMEM((3, heads), jnp.float32), pltpu.SemaphoreType.DMA((count,))],
        bytes_accessed=4 << 20,
    )
    return params, spread, loaded


def mix(parts, head_params, spread, convs, windows, norm_gain, ssm_state, steps):
    own_rows, heads, head_dim, state_size = ssm_state.shape
    block, columns = parts[0].shape
    inner, width = convs[0].shape[1], convs[1].shape[1]
    groups = width // state_size
    heads_group = heads // groups
    channels = heads_group * head_dim
    taps = convs[0].shape[0]
    count = len(parts)
    edges = (0, inner, 2 * inner, 2 * inner + width, 2 * inner + 2 * width, columns)
    terms = 1 + steps

    def body(*refs):
        part_refs = refs[:count]
        params_ref, spread_ref, *rest = refs[count:]
        conv_refs, window_refs = rest[:3], rest[3:6]
        gain_ref, state_ref, normed_ref, pre_ref, coef_ref, write_ref = rest[6:]
        total = part_refs[0][...]
        for ref in part_refs[1:]:
            total = total + ref[...].astype(jnp.float32)
        rounded = total.astype(jnp.bfloat16).astype(jnp.float32)
        pre_ref[...] = rounded[:, edges[1] : edges[4]]
        gate, *newest = [rounded[:, edges[i] : edges[i + 1]] for i in range(4)]
        bias, rate, skip = [params_ref[i : i + 1] for i in range(3)]
        step_pre = jnp.dot(
            rounded[:, edges[4] :].astype(jnp.bfloat16),
            spread_ref[...],
            preferred_element_type=jnp.float32,
        )
        step_size = jax.nn.softplus(step_pre + bias)
        decay = jnp.exp(-step_size * rate)
        gate = silu_float(gate)
        for own in range(own_rows):
            first = own * steps
            acts = []
            for which in range(3):
                taps_in = conv_refs[which][...]
                earlier = window_refs[which][own].astype(jnp.float32)
                line = [earlier[k : k + 1] for k in range(taps - 1)]
                line += [newest[which][first + s : first + s + 1] for s in range(steps)]
                acts.append(
                    [
                        silu_float(added([line[s + k] * taps_in[k : k + 1] for k in range(taps)]))
                        for s in range(steps)
                    ]
                )
            input_act, write_act, read_act = acts
            for s in range(steps):
                write_ref[pl.ds(first + s, 1), :] = write_act[s]
            sizes = [step_size[first + s : first + s + 1] for s in range(steps)]
            decays = [decay[first + s : first + s + 1] for s in range(steps)]
            fresh = [sizes[s] * input_act[s] for s in range(steps)]
            coefs = list(fresh)
            kept = jnp.ones_like(decays[0])
            for s in reversed(range(steps)):
                coefs[s] = coefs[s] * kept
                kept = kept * decays[s]
            for i, row in enumerate([kept] + coefs):
                coef_ref[own, i : i + 1, :] = row
            for g in range(groups):
                span = slice(g * channels, (g + 1) * channels)
                lanes = slice(g * state_size, (g + 1) * state_size)
                state = state_ref[own, g * heads_group : (g + 1) * heads_group]
                state = state.reshape(channels, state_size)
                reads = jnp.concatenate([read_act[s][:, lanes] for s in range(steps)], axis=0)
                high, low = [p.astype(jnp.float32) for p in split_in(reads, 2)]
                reads = jnp.concatenate([high, low], axis=0).astype(jnp.bfloat16)
                by_high, by_low = [
                    lax.dot_general(
                        reads, p, (((1,), (1,)), ((), ())), preferred_element_type=jnp.float32
                    )
                    for p in split_in(state, 2)
                ]
                product = by_high[:steps] + by_high[steps:] + by_low[:steps]
                for s in range(steps):
                    value = product[s : s + 1]
                    for j in range(s + 1):
                        overlap = jnp.sum(
                            write_act[j][:, lanes] * read_act[s][:, lanes], axis=1, keepdims=True
                        )
                        value = decays[j][:, span] * value + fresh[j][:, span] * overlap
                    value = value + skip[:, span] * input_act[s][:, span]
                    value = value * gate[first + s : first + s + 1, span]
                    mean = jnp.mean(value * value, axis=1, keepdims=True)
                    value = value * lax.rsqrt(mean + 1e-05) * gain_ref[:, span]
                    normed_ref[pl.ds(first + s, 1), span] = value.astype(jnp.bfloat16)

    return local_kernel(
        body,
        "mix",
        [
            shaped((block, inner), jnp.bfloat16),
            shaped((block, inner + 2 * width)),
            shaped((own_rows, terms, inner)),
            shaped((block, width)),
        ],
        [(a, IN_VMEM) for a in (*parts, head_params, spread, *convs, *windows, norm_gain, ssm_state)],
        bytes_accessed=MIX_COST,
    )


def renew(pre, coefs, writes, windows, ssm_state, tokens):
    steps, rows_all, depth = tokens.shape
    own_rows, heads, head_dim, state_size = ssm_state.shape
    groups = writes.shape[1] // state_size
    heads_group = heads // groups
    inner = coefs.shape[2]
    widths = [w.shape[2] for w in windows]
    kept = windows[0].shape[1]

    def body(pre_ref, coef_ref, write_ref, *rest):
        window_refs, (state_ref, tokens_ref, final_ref, current_ref) = rest[:3], rest[3:7]
        out_refs = rest[7:]
        for s in range(steps):
            current_ref[pl.ds(s * rows_all, rows_all), :] = tokens_ref[s].astype(jnp.float32)
        for own in range(own_rows):
            first = own * steps
            base = 0
            for window_ref, out_ref, width in zip(window_refs, out_refs, widths):
                line = jnp.concatenate(
                    [
                        window_ref[own].astype(jnp.float32),
                        pre_ref[pl.ds(first, steps), pl.ds(base, width)],
                    ],
                    axis=0,
                )
                out_ref[own] = line[steps:].astype(jnp.bfloat16)
                base += width
            coefs_high, coefs_low = split_in(coef_ref[own, 1 : 1 + steps, :], 2)
            writes_high, writes_low = split_in(write_ref[pl.ds(first, steps), :], 2)
            left = stacked(coefs_high, coefs_high, coefs_low)
            right = stacked(writes_high, writes_low, writes_high)
            for g in range(groups):
                fresh = lax.dot_general(
                    left[:, g * heads_group * head_dim : (g + 1) * heads_group * head_dim],
                    right[:, g * state_size : (g + 1) * state_size],
                    (((0,), (0,)), ((), ())),
                    preferred_element_type=jnp.float32,
                )
                for i in range(heads_group):
                    h = g * heads_group + i
                    kept = coef_ref[own, 0:1, pl.ds(h * head_dim, 1)]
                    final_ref[own, h] = (
                        kept * state_ref[own, h] + fresh[i * head_dim : (i + 1) * head_dim]
                    )

    return local_kernel(
        body,
        "renew",
        [shaped(ssm_state.shape), shaped((steps * rows_all, depth))]
        + [shaped(w.shape, jnp.bfloat16) for w in windows],
        [(a, IN_VMEM) for a in (pre, coefs, writes, *windows, ssm_state, tokens)],
        bytes_accessed=4 << 20,
    )


def fetch(array, after):
    def body(source, _, target, sem):
        copy = pltpu.make_async_copy(source, target, sem)
        copy.start()
        copy.wait()

    return local_kernel(
        body,
        "fetch",
        shaped(array.shape, array.dtype),
        [(array, IN_HBM), (after, IN_VMEM)],
        [pltpu.SemaphoreType.DMA],
        bytes_accessed=8 << 20,
    )


def project_out(normed, out_proj, steps):
    owners = len(normed)
    block, inner = normed[0].shape
    own_rows = block // steps
    rows = own_rows * owners

    def body(*refs):
        weights_ref, out_ref, sent_ref, lhs = refs[owners:]
        for slot in range(owners):
            owner = owner_of(slot, "expert")
            values = refs[slot][...].astype(jnp.float32)
            for own in range(own_rows):
                for s in range(steps):
                    row = s * rows + owner * own_rows + own
                    lhs[pl.ds(row, 1), :] = values[own * steps + s : own * steps + s + 1]
        total = jnp.dot(
            lhs[...].astype(jnp.bfloat16), weights_ref[...], preferred_element_type=jnp.float32
        )
        out_ref[...] = total
        sent_ref[...] = total.astype(jnp.bfloat16)

    return local_kernel(
        body,
        "project_out",
        sent_narrow((rows * steps, out_proj.shape[1]), 2),
        [(a, IN_VMEM) for a in (*normed, out_proj)],
        [pltpu.VMEM((rows * steps, inner), jnp.float32)],
        bytes_accessed=4 << 20,
    )


def experts(moe_in, chosen, gates, expert_up, expert_down):
    owners = len(moe_in)
    many, width = moe_in[0].shape
    steps, rows, _ = chosen.shape
    local_experts, _, hidden_width = expert_up.shape

    def body(*refs):
        chosen_ref, gates_ref, up_ref, down_ref = refs[owners : owners + 4]
        outs, hidden_ref = refs[owners + 4 : -1], refs[-1]
        first = lax.axis_index("expert") * local_experts

        def span(slot):
            start = owner_of(slot, "expert") * width
            return pl.ds(pl.multiple_of(start, width) if pairwise("expert") else start, width)

        row_weights = []
        for e in range(local_experts):
            total = jnp.zeros((many, hidden_width), jnp.float32)
            for slot in range(owners):
                total += jnp.dot(
                    refs[slot][...], up_ref[e, span(slot), :], preferred_element_type=jnp.float32
                )
            total = jnp.maximum(total, 0.0)
            hidden_ref[e] = (total * total).astype(jnp.bfloat16)
            row_weights.append(
                jnp.concatenate(
                    [
                        jnp.sum(
                            jnp.where(chosen_ref[s] == first + e, gates_ref[s], 0.0),
                            axis=1,
                            keepdims=True,
                        )
                        for s in range(steps)
                    ],
                    axis=0,
                )
            )
        for slot in range(owners):
            total = jnp.zeros((many, width), jnp.float32)
            for e in range(local_experts):
                total += row_weights[e] * jnp.dot(
                    hidden_ref[e], down_ref[e, :, span(slot)], preferred_element_type=jnp.float32
                )
            outs[slot][...] = total.astype(outs[slot].dtype)

    return local_kernel(
        body,
        "experts",
        sent_narrow((many, width), owners),
        [
            (a, IN_VMEM)
            for a in (*moe_in, chosen, gates, resident(expert_up), resident(expert_down))
        ],
        [pltpu.VMEM((local_experts, many, hidden_width), jnp.bfloat16)],
        bytes_accessed=16 << 20,
    )


def finish(parts, shape):
    steps, rows, _ = shape

    def body(*refs):
        total = added([ref[...] for ref in refs[:-1]])
        for s in range(steps):
            refs[-1][s] = total[s * rows : (s + 1) * rows].astype(jnp.bfloat16)

    return local_kernel(body, "finish", shaped(shape, jnp.bfloat16), [(p, IN_VMEM) for p in parts])


def per_device(
    tokens,
    proj_gate,
    proj_input,
    proj_write,
    proj_read,
    proj_step,
    conv_input,
    conv_write,
    conv_read,
    window_input,
    window_write,
    window_read,
    step_bias,
    decay_log,
    skip_gain,
    norm_gain,
    ssm_state,
    out_proj,
    expert_up,
    expert_down,
    expert_ids,
    route_gates,
):
    steps = tokens.shape[0]
    inner = conv_input.shape[1]
    windows = (window_input, window_write, window_read)
    projected = project(
        lax.axis_size("expert"),
        tokens,
        (proj_gate, proj_input, proj_write, proj_read),
        proj_step.T,
    )
    head_params, spread, loaded = prepare(
        *[p.reshape(1, -1) for p in (step_bias, decay_log, skip_gain)],
        inner,
        (conv_input, conv_write, conv_read, *windows, norm_gain.reshape(1, -1), ssm_state)
        + (tokens, expert_ids, route_gates),
    )
    convs, windows = loaded[:3], loaded[3:6]
    norm_gain, ssm_state, tokens, expert_ids, route_gates = loaded[6:]
    normed, pre, coefs, writes = mix(
        scatter_parts(projected, "expert"),
        head_params,
        spread,
        convs,
        windows,
        norm_gain,
        ssm_state,
        steps,
    )
    partial, sent = project_out(gather(normed, "expert"), fetch(out_proj, writes), steps)
    ssm_final, current, *finals = renew(pre, coefs, writes, windows, ssm_state, tokens)
    residual = added([current] + sum_parts(partial, "tensor", sent))
    moe_in = gather(residual.astype(jnp.bfloat16), "expert")
    moe_sum = experts(moe_in, expert_ids, route_gates, expert_up, expert_down)
    moe_sum = added(scatter_parts(moe_sum, "expert"))
    mixed_out = finish([residual] + sum_parts(moe_sum, "tensor", moe_sum.astype(jnp.bfloat16)), tokens.shape)
    return (mixed_out, ssm_final, *finals)


def solution(mesh):
    placed = (
        P(None, "groups", "expert"),
        P("expert", "tensor"),
        P("expert", "tensor"),
        P("expert", "tensor"),
        P("expert", "tensor"),
        P("expert", "tensor"),
        P(None, "tensor"),
        P(None, "tensor"),
        P(None, "tensor"),
        P(("groups", "expert"), None, "tensor"),
        P(("groups", "expert"), None, "tensor"),
        P(("groups", "expert"), None, "tensor"),
        P("tensor"),
        P("tensor"),
        P("tensor"),
        P("tensor"),
        P(("groups", "expert"), "tensor", None, None),
        P("tensor", "expert"),
        P("expert", None, "tensor"),
        P("expert", "tensor", None),
        P(None, "groups", None),
        P(None, "groups", None),
    )
    return jax.shard_map(
        per_device,
        mesh=mesh,
        in_specs=placed,
        out_specs=(
            P(None, "groups", "expert"),
            P(("groups", "expert"), "tensor", None, None),
            P(("groups", "expert"), None, "tensor"),
            P(("groups", "expert"), None, "tensor"),
            P(("groups", "expert"), None, "tensor"),
        ),
        check_vma=False,
    )
```

```python
import jax
import jax.numpy as jnp
from jax import lax
from jax.experimental import pallas as pl
from jax.experimental.pallas import tpu as pltpu
from jax.sharding import PartitionSpec as P


def silu_float(values):
    return values / (1.0 + jnp.exp(-values))


def pairwise(axis):
    size = lax.axis_size(axis)
    return size <= 4 and size & (size - 1) == 0


def swap(values, axis, distance):
    size = lax.axis_size(axis)
    return lax.ppermute(values, axis, [(i, i ^ distance) for i in range(size)])


def gather(values, axis):
    size = lax.axis_size(axis)
    if not pairwise(axis):
        held = lax.all_gather(values, axis, axis=0)
        return [held[j] for j in range(size)]
    return [values] + [swap(values, axis, d) for d in range(1, size)]


def sum_parts(values, axis, sent, order):
    if not pairwise(axis):
        return [lax.psum(values, axis)]
    if lax.axis_size(axis) != 4:
        return [values] + [swap(sent, axis, d) for d in range(1, lax.axis_size(axis))]
    return [values] + [lax.ppermute(sent, axis, list(enumerate(p))) for p in order]


def scatter_parts(blocks, axis):
    if not pairwise(axis):
        blocks = jnp.stack([block.astype(jnp.float32) for block in blocks])
        return [lax.psum_scatter(blocks, axis, scatter_dimension=0, tiled=False)]
    return [blocks[0]] + [swap(blocks[d], axis, d) for d in reversed(range(1, len(blocks)))]


def added(parts):
    total = parts[0]
    for part in parts[1:]:
        total = total + part.astype(total.dtype)
    return total


def owner_of(slot, axis):
    return lax.axis_index(axis) ^ slot if pairwise(axis) else slot


VMEM_LIMIT = 16 * 1024 * 1024
IN_VMEM = pl.BlockSpec(memory_space=pltpu.VMEM)
IN_HBM = pl.BlockSpec(memory_space=pltpu.HBM)
CHUNK = 512 * 1024
MIX_COST = 4 << 20
FIRST = 4
NEAR = 1


def local_kernel(body, name, out_shape, ins, scratch=(), bytes_accessed=1 << 20):
    return pl.pallas_call(
        body,
        out_shape=out_shape,
        in_specs=[spec for _, spec in ins],
        out_specs=jax.tree.map(lambda _: IN_VMEM, out_shape),
        scratch_shapes=list(scratch),
        compiler_params=pltpu.CompilerParams(vmem_limit_bytes=VMEM_LIMIT),
        cost_estimate=pl.CostEstimate(
            flops=bytes_accessed, bytes_accessed=bytes_accessed, transcendentals=0
        ),
        name=name,
    )(*[held(array, spec) for array, spec in ins])


def held(array, spec):
    if spec is IN_HBM:
        return pltpu.with_memory_space_constraint(array, pltpu.HBM)
    return array


def resident(array):
    return pltpu.with_memory_space_constraint(array, pltpu.VMEM)


def shaped(shape, dtype=jnp.float32):
    return jax.ShapeDtypeStruct(tuple(shape), dtype)


def sent_narrow(shape, slots):
    return [shaped(shape)] + [shaped(shape, jnp.bfloat16)] * (slots - 1)


def project(owners, tokens, weights, step_weights):
    steps, rows, depth = tokens.shape
    own_rows = rows // owners
    widths = [w.shape[1] for w in weights]
    heads = step_weights.shape[0]
    columns = sum(widths) + heads
    block = own_rows * steps
    pieces = []
    for index, width in enumerate(widths):
        size = max(16, min(depth, CHUNK // width))
        pieces += [(index, start, min(size, depth - start)) for start in range(0, depth, size)]
    bases = [sum(widths[:index]) for index in range(len(widths))]
    count = len(weights)

    def body(*refs):
        tokens_ref, step_ref = refs[:2]
        weight_refs = refs[2 : 2 + count]
        outs = refs[2 + count : 2 + count + owners]
        tokens_in, step_in, wide, lhs, sems, *weights_in = refs[2 + count + owners :]
        first = [
            pltpu.make_async_copy(tokens_ref, tokens_in, sems.at[0]),
            pltpu.make_async_copy(step_ref, step_in, sems.at[1]),
        ]
        copies = [
            pltpu.make_async_copy(
                weight_refs[index].at[pl.ds(start, size)],
                weights_in[index].at[pl.ds(start, size)],
                sems.at[2 + i],
            )
            for i, (index, start, size) in enumerate(pieces)
        ]
        for copy in first + copies:
            copy.start()
        first[0].wait()
        wide[...] = tokens_in[...].astype(jnp.float32)
        for slot in range(owners):
            owner = owner_of(slot, "expert")
            for own in range(own_rows):
                for s in range(steps):
                    row = slot * block + own * steps + s
                    lhs[pl.ds(row, 1), :] = wide[s, pl.ds(owner * own_rows + own, 1), :]
        rows_in = lhs[...].astype(jnp.bfloat16)

        def put(place, size, result):
            for slot in range(owners):
                part = result[slot * block : (slot + 1) * block]
                outs[slot][:, pl.ds(place, size)] = part.astype(outs[slot].dtype)

        first[1].wait()
        put(
            columns - heads,
            heads,
            lax.dot_general(
                rows_in,
                step_in[...],
                (((1,), (1,)), ((), ())),
                preferred_element_type=jnp.float32,
            ),
        )
        total = None
        for copy, (index, start, size) in zip(copies, pieces):
            copy.wait()
            product = jnp.dot(
                rows_in[:, start : start + size],
                weights_in[index][pl.ds(start, size)],
                preferred_element_type=jnp.float32,
            )
            total = product if start == 0 else total + product
            if start + size == depth:
                put(bases[index], widths[index], total)

    return local_kernel(
        body,
        "project",
        sent_narrow((block, columns), owners),
        [(tokens, IN_HBM), (step_weights, IN_HBM)] + [(w, IN_HBM) for w in weights],
        [
            pltpu.VMEM(tokens.shape, jnp.bfloat16),
            pltpu.VMEM(step_weights.shape, jnp.bfloat16),
            pltpu.VMEM(tokens.shape, jnp.float32),
            pltpu.VMEM((owners * block, depth), jnp.float32),
            pltpu.SemaphoreType.DMA((2 + len(pieces),)),
        ]
        + [pltpu.VMEM(w.shape, jnp.bfloat16) for w in weights],
        bytes_accessed=10 << 20,
    )


def split_in(values, terms):
    parts = []
    for _ in range(terms):
        part = values.astype(jnp.bfloat16)
        parts.append(part)
        values = values - part.astype(jnp.float32)
    return parts


def stacked(*parts):
    rows = sum(part.shape[0] for part in parts)
    parts = [part.astype(jnp.float32) for part in parts]
    parts.append(jnp.zeros((-rows % 8, parts[0].shape[1]), jnp.float32))
    return jnp.concatenate(parts, axis=0).astype(jnp.bfloat16)


def prepare(step_bias, decay_log, skip_gain, inner, arrays, weights, rows_first):
    heads = step_bias.shape[1]
    head_dim = inner // heads
    count = 4 + len(arrays)
    wanted = [shaped(a.shape, a.dtype) for a in arrays]
    wanted.append(shaped((rows_first, weights.shape[1]), weights.dtype))

    def body(*refs):
        sources, (params_ref, spread_ref), outs = refs[:count], refs[count : count + 2], refs[count + 2 :]
        loaded, sems = outs[:-2], outs[-1]
        rows_ref = outs[-2]
        sources = [*sources[:-1], sources[-1].at[pl.ds(0, rows_first)]]
        targets = [rows_ref.at[pl.ds(i, 1)] for i in range(3)] + list(loaded)
        copies = [
            pltpu.make_async_copy(source, target, sems.at[i])
            for i, (source, target) in enumerate(zip(sources, targets))
        ]
        for copy in copies:
            copy.start()
        head = lax.broadcasted_iota(jnp.int32, (heads, inner), 0) * head_dim
        channel = lax.broadcasted_iota(jnp.int32, (heads, inner), 1)
        inside = (channel >= head) & (channel < head + head_dim)
        spread = jnp.where(inside, 1.0, 0.0).astype(jnp.bfloat16)
        spread_ref[...] = spread
        for copy in copies[:3]:
            copy.wait()
        rows = rows_ref[...]
        rows = jnp.concatenate([rows[0:1], jnp.exp(rows[1:2]), rows[2:3]], axis=0)
        total = jnp.zeros((3, inner), jnp.float32)
        for part in reversed(split_in(rows, 3)):
            total += jnp.dot(part, spread, preferred_element_type=jnp.float32)
        params_ref[...] = total
        for copy in copies[3:]:
            copy.wait()

    params, spread, *loaded = local_kernel(
        body,
        "prepare",
        [shaped((3, inner)), shaped((heads, inner), jnp.bfloat16)]
        + wanted,
        [(a, IN_HBM) for a in (step_bias, decay_log, skip_gain, *arrays, weights)],
        [pltpu.VMEM((3, heads), jnp.float32), pltpu.SemaphoreType.DMA((count,))],
        bytes_accessed=4 << 20,
    )
    return params, spread, loaded


def mix(parts, head_params, spread, convs, windows, norm_gain, ssm_state, steps):
    own_rows, heads, head_dim, state_size = ssm_state.shape
    block, columns = parts[0].shape
    inner, width = convs[0].shape[1], convs[1].shape[1]
    groups = width // state_size
    heads_group = heads // groups
    channels = heads_group * head_dim
    taps = convs[0].shape[0]
    count = len(parts)
    edges = (0, inner, 2 * inner, 2 * inner + width, 2 * inner + 2 * width, columns)
    terms = 1 + steps

    def body(*refs):
        part_refs = refs[:count]
        params_ref, spread_ref, *rest = refs[count:]
        conv_refs, window_refs = rest[:3], rest[3:6]
        gain_ref, state_ref, normed_ref, pre_ref, coef_ref, write_ref = rest[6:]
        total = part_refs[0][...]
        for ref in part_refs[1:]:
            total = total + ref[...].astype(jnp.float32)
        rounded = total.astype(jnp.bfloat16).astype(jnp.float32)
        pre_ref[...] = rounded[:, edges[1] : edges[4]]
        gate, *newest = [rounded[:, edges[i] : edges[i + 1]] for i in range(4)]
        bias, rate, skip = [params_ref[i : i + 1] for i in range(3)]
        step_pre = jnp.dot(
            rounded[:, edges[4] :].astype(jnp.bfloat16),
            spread_ref[...],
            preferred_element_type=jnp.float32,
        )
        step_size = jax.nn.softplus(step_pre + bias)
        decay = jnp.exp(-step_size * rate)
        gate = silu_float(gate)
        for own in range(own_rows):
            first = own * steps
            acts = []
            for which in range(3):
                taps_in = conv_refs[which][...]
                earlier = window_refs[which][own].astype(jnp.float32)
                line = [earlier[k : k + 1] for k in range(taps - 1)]
                line += [newest[which][first + s : first + s + 1] for s in range(steps)]
                acts.append(
                    [
                        silu_float(added([line[s + k] * taps_in[k : k + 1] for k in range(taps)]))
                        for s in range(steps)
                    ]
                )
            input_act, write_act, read_act = acts
            for s in range(steps):
                write_ref[pl.ds(first + s, 1), :] = write_act[s]
            sizes = [step_size[first + s : first + s + 1] for s in range(steps)]
            decays = [decay[first + s : first + s + 1] for s in range(steps)]
            fresh = [sizes[s] * input_act[s] for s in range(steps)]
            coefs = list(fresh)
            kept = jnp.ones_like(decays[0])
            for s in reversed(range(steps)):
                coefs[s] = coefs[s] * kept
                kept = kept * decays[s]
            for i, row in enumerate([kept] + coefs):
                coef_ref[own, i : i + 1, :] = row
            for g in range(groups):
                span = slice(g * channels, (g + 1) * channels)
                lanes = slice(g * state_size, (g + 1) * state_size)
                state = state_ref[own, g * heads_group : (g + 1) * heads_group]
                state = state.reshape(channels, state_size)
                reads = jnp.concatenate([read_act[s][:, lanes] for s in range(steps)], axis=0)
                high, low = [p.astype(jnp.float32) for p in split_in(reads, 2)]
                reads = jnp.concatenate([high, low], axis=0).astype(jnp.bfloat16)
                by_high, by_low = [
                    lax.dot_general(
                        reads, p, (((1,), (1,)), ((), ())), preferred_element_type=jnp.float32
                    )
                    for p in split_in(state, 2)
                ]
                product = by_high[:steps] + by_high[steps:] + by_low[:steps]
                for s in range(steps):
                    value = product[s : s + 1]
                    for j in range(s + 1):
                        overlap = jnp.sum(
                            write_act[j][:, lanes] * read_act[s][:, lanes], axis=1, keepdims=True
                        )
                        value = decays[j][:, span] * value + fresh[j][:, span] * overlap
                    value = value + skip[:, span] * input_act[s][:, span]
                    value = value * gate[first + s : first + s + 1, span]
                    mean = jnp.mean(value * value, axis=1, keepdims=True)
                    value = value * lax.rsqrt(mean + 1e-05) * gain_ref[:, span]
                    normed_ref[pl.ds(first + s, 1), span] = value.astype(jnp.bfloat16)

    return local_kernel(
        body,
        "mix",
        [
            shaped((block, inner), jnp.bfloat16),
            shaped((block, inner + 2 * width)),
            shaped((own_rows, terms, inner)),
            shaped((block, width)),
        ],
        [(a, IN_VMEM) for a in (*parts, head_params, spread, *convs, *windows, norm_gain, ssm_state)],
        bytes_accessed=MIX_COST,
    )


def renew(pre, coefs, writes, windows, ssm_state, tokens):
    steps, rows_all, depth = tokens.shape
    own_rows, heads, head_dim, state_size = ssm_state.shape
    groups = writes.shape[1] // state_size
    heads_group = heads // groups
    inner = coefs.shape[2]
    widths = [w.shape[2] for w in windows]
    kept = windows[0].shape[1]

    def body(pre_ref, coef_ref, write_ref, *rest):
        window_refs, (state_ref, tokens_ref, final_ref, current_ref) = rest[:3], rest[3:7]
        out_refs = rest[7:]
        for s in range(steps):
            current_ref[pl.ds(s * rows_all, rows_all), :] = tokens_ref[s].astype(jnp.float32)
        for own in range(own_rows):
            first = own * steps
            base = 0
            for window_ref, out_ref, width in zip(window_refs, out_refs, widths):
                line = jnp.concatenate(
                    [
                        window_ref[own].astype(jnp.float32),
                        pre_ref[pl.ds(first, steps), pl.ds(base, width)],
                    ],
                    axis=0,
                )
                out_ref[own] = line[steps:].astype(jnp.bfloat16)
                base += width
            coefs_high, coefs_low = split_in(coef_ref[own, 1 : 1 + steps, :], 2)
            writes_high, writes_low = split_in(write_ref[pl.ds(first, steps), :], 2)
            left = stacked(coefs_high, coefs_high, coefs_low)
            right = stacked(writes_high, writes_low, writes_high)
            for g in range(groups):
                fresh = lax.dot_general(
                    left[:, g * heads_group * head_dim : (g + 1) * heads_group * head_dim],
                    right[:, g * state_size : (g + 1) * state_size],
                    (((0,), (0,)), ((), ())),
                    preferred_element_type=jnp.float32,
                )
                for i in range(heads_group):
                    h = g * heads_group + i
                    kept = coef_ref[own, 0:1, pl.ds(h * head_dim, 1)]
                    final_ref[own, h] = (
                        kept * state_ref[own, h] + fresh[i * head_dim : (i + 1) * head_dim]
                    )

    return local_kernel(
        body,
        "renew",
        [shaped(ssm_state.shape), shaped((steps * rows_all, depth))]
        + [shaped(w.shape, jnp.bfloat16) for w in windows],
        [(a, IN_VMEM) for a in (pre, coefs, writes, *windows, ssm_state, tokens)],
        bytes_accessed=4 << 20,
    )


def fetch(array, start, after):
    rows = array.shape[0] - start

    def body(source, _, target, sem):
        copy = pltpu.make_async_copy(source.at[pl.ds(start, rows)], target, sem)
        copy.start()
        copy.wait()

    return local_kernel(
        body,
        "fetch",
        shaped((rows, array.shape[1]), array.dtype),
        [(array, IN_HBM), (after, IN_VMEM)],
        [pltpu.SemaphoreType.DMA],
        bytes_accessed=8 << 20,
    )


def project_out(normed, parts, steps):
    owners = len(normed)
    block, inner = normed[0].shape
    own_rows = block // steps
    rows = own_rows * owners

    def body(*refs):
        out_ref, sent_ref, lhs = refs[owners + len(parts) :]
        for slot in range(owners):
            owner = owner_of(slot, "expert")
            values = refs[slot][...].astype(jnp.float32)
            for own in range(own_rows):
                for s in range(steps):
                    row = s * rows + owner * own_rows + own
                    lhs[pl.ds(row, 1), :] = values[own * steps + s : own * steps + s + 1]
        products = []
        base = 0
        for ref in refs[owners : owners + len(parts)]:
            values = lhs[:, pl.ds(base, ref.shape[0])].astype(jnp.bfloat16)
            products.append(jnp.dot(values, ref[...], preferred_element_type=jnp.float32))
            base += ref.shape[0]
        total = added(products)
        out_ref[...] = total
        sent_ref[...] = total.astype(jnp.bfloat16)

    return local_kernel(
        body,
        "project_out",
        sent_narrow((rows * steps, parts[0].shape[1]), 2),
        [(a, IN_VMEM) for a in (*normed, *parts)],
        [pltpu.VMEM((rows * steps, inner), jnp.float32)],
        bytes_accessed=4 << 20,
    )


def slot_rows(slot, width):
    start = owner_of(slot, "expert") * width
    return pl.ds(pl.multiple_of(start, width) if pairwise("expert") else start, width)


def expert_near(moe_in, expert_up):
    count = len(moe_in)
    many, width = moe_in[0].shape
    local_experts, _, hidden_width = expert_up.shape

    def body(*refs):
        up_ref, out_ref = refs[count:]
        for e in range(local_experts):
            out_ref[e] = added(
                [
                    jnp.dot(
                        refs[slot][...],
                        up_ref[e, slot_rows(slot, width), :],
                        preferred_element_type=jnp.float32,
                    )
                    for slot in range(count)
                ]
            )

    return local_kernel(
        body,
        "expert_near",
        shaped((local_experts, many, hidden_width)),
        [(a, IN_VMEM) for a in (*moe_in, expert_up)],
        bytes_accessed=4 << 20,
    )


def row_weights(chosen_ref, gates_ref, local_experts):
    first = lax.axis_index("expert") * local_experts
    steps = chosen_ref.shape[0]
    return [
        jnp.concatenate(
            [
                jnp.sum(
                    jnp.where(chosen_ref[s] == first + e, gates_ref[s], 0.0),
                    axis=1,
                    keepdims=True,
                )
                for s in range(steps)
            ],
            axis=0,
        )
        for e in range(local_experts)
    ]


def gated_sum(hidden_ref, weights, down_ref, columns):
    return added(
        [
            weights[e]
            * jnp.dot(
                hidden_ref[e], down_ref[e, :, columns], preferred_element_type=jnp.float32
            )
            for e in range(len(weights))
        ]
    )


def experts_far(near, moe_in, chosen, gates, expert_up, expert_down, owners):
    count = len(moe_in)
    many, width = moe_in[0].shape
    local_experts, _, hidden_width = expert_up.shape
    far = range(1, owners)

    def body(*refs):
        near_ref, chosen_ref, gates_ref, up_ref, down_ref, hidden_ref, *outs = refs[count:]
        for e in range(local_experts):
            total = near_ref[e]
            for i in range(count):
                total += jnp.dot(
                    refs[i][...],
                    up_ref[e, slot_rows(owners - count + i, width), :],
                    preferred_element_type=jnp.float32,
                )
            total = jnp.maximum(total, 0.0)
            hidden_ref[e] = (total * total).astype(jnp.bfloat16)
        weights = row_weights(chosen_ref, gates_ref, local_experts)
        for slot, out in zip(far, outs):
            total = gated_sum(hidden_ref, weights, down_ref, slot_rows(slot, width))
            out[...] = total.astype(out.dtype)

    hidden, *outs = local_kernel(
        body,
        "experts_far",
        [shaped((local_experts, many, hidden_width), jnp.bfloat16)]
        + sent_narrow((many, width), 1 + len(far))[1:],
        [(a, IN_VMEM) for a in (*moe_in, near, chosen, gates, expert_up, expert_down)],
        bytes_accessed=16 << 20,
    )
    return hidden, outs


def experts_close(hidden, chosen, gates, expert_down, owners):
    local_experts, many, _ = hidden.shape
    width = expert_down.shape[2] // owners

    def body(hidden_ref, chosen_ref, gates_ref, down_ref, *outs):
        weights = row_weights(chosen_ref, gates_ref, local_experts)
        for slot, out in enumerate(outs):
            total = gated_sum(hidden_ref, weights, down_ref, slot_rows(slot, width))
            out[...] = total.astype(out.dtype)

    return local_kernel(
        body,
        "experts_close",
        sent_narrow((many, width), 1),
        [(a, IN_VMEM) for a in (hidden, chosen, gates, expert_down)],
        bytes_accessed=4 << 20,
    )


def finish(parts, shape):
    steps, rows, _ = shape

    def body(*refs):
        total = added([ref[...] for ref in refs[:-1]])
        for s in range(steps):
            refs[-1][s] = total[s * rows : (s + 1) * rows].astype(jnp.bfloat16)

    return local_kernel(body, "finish", shaped(shape, jnp.bfloat16), [(p, IN_VMEM) for p in parts])


def per_device(
    tokens,
    proj_gate,
    proj_input,
    proj_write,
    proj_read,
    proj_step,
    conv_input,
    conv_write,
    conv_read,
    window_input,
    window_write,
    window_read,
    step_bias,
    decay_log,
    skip_gain,
    norm_gain,
    ssm_state,
    out_proj,
    expert_up,
    expert_down,
    expert_ids,
    route_gates,
):
    steps = tokens.shape[0]
    inner = conv_input.shape[1]
    windows = (window_input, window_write, window_read)
    projected = project(
        lax.axis_size("expert"),
        tokens,
        (proj_gate, proj_input, proj_write, proj_read),
        proj_step.T,
    )
    head_params, spread, loaded = prepare(
        *[p.reshape(1, -1) for p in (step_bias, decay_log, skip_gain)],
        inner,
        (conv_input, conv_write, conv_read, *windows, norm_gain.reshape(1, -1), ssm_state)
        + (tokens, expert_ids, route_gates),
        out_proj,
        inner // FIRST,
    )
    convs, windows = loaded[:3], loaded[3:6]
    norm_gain, ssm_state, tokens, expert_ids, route_gates, out_first = loaded[6:]
    normed, pre, coefs, writes = mix(
        scatter_parts(projected, "expert"),
        head_params,
        spread,
        convs,
        windows,
        norm_gain,
        ssm_state,
        steps,
    )
    partial, sent = project_out(gather(normed, "expert"), (out_first, fetch(out_proj, inner // FIRST, writes)), steps)
    ssm_final, current, *finals = renew(pre, coefs, writes, windows, ssm_state, tokens)
    residual = added([current] + sum_parts(partial, "tensor", sent, ((2, 0, 3, 1), (3, 2, 1, 0), (1, 3, 0, 2))))
    moe_in = gather(residual.astype(jnp.bfloat16), "expert")
    expert_up, expert_down = resident(expert_up), resident(expert_down)
    near = expert_near(moe_in[:NEAR], expert_up)
    owners = len(moe_in)
    hidden, far = experts_far(
        near, moe_in[NEAR:], expert_ids, route_gates, expert_up, expert_down, owners
    )
    moe_sum = [*experts_close(hidden, expert_ids, route_gates, expert_down, owners), *far]
    moe_sum = added(scatter_parts(moe_sum, "expert"))
    mixed_out = finish([residual] + sum_parts(moe_sum, "tensor", moe_sum.astype(jnp.bfloat16), ((1, 0, 3, 2), (2, 3, 0, 1), (3, 2, 1, 0))), tokens.shape)
    return (mixed_out, ssm_final, *finals)


def solution(mesh):
    placed = (
        P(None, "groups", "expert"),
        P("expert", "tensor"),
        P("expert", "tensor"),
        P("expert", "tensor"),
        P("expert", "tensor"),
        P("expert", "tensor"),
        P(None, "tensor"),
        P(None, "tensor"),
        P(None, "tensor"),
        P(("groups", "expert"), None, "tensor"),
        P(("groups", "expert"), None, "tensor"),
        P(("groups", "expert"), None, "tensor"),
        P("tensor"),
        P("tensor"),
        P("tensor"),
        P("tensor"),
        P(("groups", "expert"), "tensor", None, None),
        P("tensor", "expert"),
        P("expert", None, "tensor"),
        P("expert", "tensor", None),
        P(None, "groups", None),
        P(None, "groups", None),
    )
    return jax.shard_map(
        per_device,
        mesh=mesh,
        in_specs=placed,
        out_specs=(
            P(None, "groups", "expert"),
            P(("groups", "expert"), "tensor", None, None),
            P(("groups", "expert"), None, "tensor"),
            P(("groups", "expert"), None, "tensor"),
            P(("groups", "expert"), None, "tensor"),
        ),
        check_vma=False,
    )
```

```python
import jax
import jax.numpy as jnp
from jax import lax
from jax.experimental import pallas as pl
from jax.experimental.pallas import tpu as pltpu
from jax.sharding import PartitionSpec as P


def silu_float(values):
    return values / (1.0 + jnp.exp(-values))


def pairwise(axis):
    size = lax.axis_size(axis)
    return size <= 4 and size & (size - 1) == 0


def swap(values, axis, distance):
    size = lax.axis_size(axis)
    return lax.ppermute(values, axis, [(i, i ^ distance) for i in range(size)])


def gather(values, axis):
    size = lax.axis_size(axis)
    if not pairwise(axis):
        held = lax.all_gather(values, axis, axis=0)
        return [held[j] for j in range(size)]
    return [values] + [swap(values, axis, d) for d in range(1, size)]


def sum_parts(values, axis, sent, order):
    if not pairwise(axis):
        return [lax.psum(values, axis)]
    if lax.axis_size(axis) != 4:
        return [values] + [swap(sent, axis, d) for d in range(1, lax.axis_size(axis))]
    return [values] + [lax.ppermute(sent, axis, list(enumerate(p))) for p in order]


def scatter_parts(blocks, axis):
    if not pairwise(axis):
        blocks = jnp.stack([block.astype(jnp.float32) for block in blocks])
        return [lax.psum_scatter(blocks, axis, scatter_dimension=0, tiled=False)]
    return [blocks[0]] + [swap(blocks[d], axis, d) for d in (2, 3, 1) if d < len(blocks)]


def added(parts):
    total = parts[0]
    for part in parts[1:]:
        total = total + part.astype(total.dtype)
    return total


def owner_of(slot, axis):
    return lax.axis_index(axis) ^ slot if pairwise(axis) else slot


VMEM_LIMIT = 16 * 1024 * 1024
IN_VMEM = pl.BlockSpec(memory_space=pltpu.VMEM)
IN_HBM = pl.BlockSpec(memory_space=pltpu.HBM)
CHUNK = 512 * 1024
FIRST = 4
NEAR = 1


def local_kernel(body, name, out_shape, ins, scratch=(), bytes_accessed=1 << 20):
    return pl.pallas_call(
        body,
        out_shape=out_shape,
        in_specs=[spec for _, spec in ins],
        out_specs=jax.tree.map(lambda _: IN_VMEM, out_shape),
        scratch_shapes=list(scratch),
        compiler_params=pltpu.CompilerParams(vmem_limit_bytes=VMEM_LIMIT),
        cost_estimate=pl.CostEstimate(
            flops=bytes_accessed, bytes_accessed=bytes_accessed, transcendentals=0
        ),
        name=name,
    )(*[held(array, spec) for array, spec in ins])


def held(array, spec):
    if spec is IN_HBM:
        return pltpu.with_memory_space_constraint(array, pltpu.HBM)
    return array


def resident(array):
    return pltpu.with_memory_space_constraint(array, pltpu.VMEM)


def shaped(shape, dtype=jnp.float32):
    return jax.ShapeDtypeStruct(tuple(shape), dtype)


def sent_narrow(shape, slots):
    return [shaped(shape)] + [shaped(shape, jnp.bfloat16)] * (slots - 1)


def project(owners, tokens, weights, step_weights):
    steps, rows, depth = tokens.shape
    own_rows = rows // owners
    widths = [w.shape[1] for w in weights]
    heads = step_weights.shape[0]
    columns = sum(widths) + heads
    block = own_rows * steps
    pieces = []
    for index, width in enumerate(widths):
        size = max(16, min(depth, CHUNK // width))
        pieces += [(index, start, min(size, depth - start)) for start in range(0, depth, size)]
    bases = [sum(widths[:index]) for index in range(len(widths))]
    count = len(weights)

    def body(*refs):
        tokens_ref, step_ref = refs[:2]
        weight_refs = refs[2 : 2 + count]
        outs = refs[2 + count : 2 + count + owners]
        tokens_in, step_in, wide, lhs, sems, *weights_in = refs[2 + count + owners :]
        first = [
            pltpu.make_async_copy(tokens_ref, tokens_in, sems.at[0]),
            pltpu.make_async_copy(step_ref, step_in, sems.at[1]),
        ]
        copies = [
            pltpu.make_async_copy(
                weight_refs[index].at[pl.ds(start, size)],
                weights_in[index].at[pl.ds(start, size)],
                sems.at[2 + i],
            )
            for i, (index, start, size) in enumerate(pieces)
        ]
        for copy in first + copies:
            copy.start()
        first[0].wait()
        wide[...] = tokens_in[...].astype(jnp.float32)
        for slot in range(owners):
            owner = owner_of(slot, "expert")
            for own in range(own_rows):
                for s in range(steps):
                    row = slot * block + own * steps + s
                    lhs[pl.ds(row, 1), :] = wide[s, pl.ds(owner * own_rows + own, 1), :]
        rows_in = lhs[...].astype(jnp.bfloat16)

        def put(place, size, result):
            for slot in range(owners):
                part = result[slot * block : (slot + 1) * block]
                outs[slot][:, pl.ds(place, size)] = part.astype(outs[slot].dtype)

        first[1].wait()
        put(
            columns - heads,
            heads,
            lax.dot_general(
                rows_in,
                step_in[...],
                (((1,), (1,)), ((), ())),
                preferred_element_type=jnp.float32,
            ),
        )
        total = None
        for copy, (index, start, size) in zip(copies, pieces):
            copy.wait()
            product = jnp.dot(
                rows_in[:, start : start + size],
                weights_in[index][pl.ds(start, size)],
                preferred_element_type=jnp.float32,
            )
            total = product if start == 0 else total + product
            if start + size == depth:
                put(bases[index], widths[index], total)

    return local_kernel(
        body,
        "project",
        sent_narrow((block, columns), owners),
        [(tokens, IN_HBM), (step_weights, IN_HBM)] + [(w, IN_HBM) for w in weights],
        [
            pltpu.VMEM(tokens.shape, jnp.bfloat16),
            pltpu.VMEM(step_weights.shape, jnp.bfloat16),
            pltpu.VMEM(tokens.shape, jnp.float32),
            pltpu.VMEM((owners * block, depth), jnp.float32),
            pltpu.SemaphoreType.DMA((2 + len(pieces),)),
        ]
        + [pltpu.VMEM(w.shape, jnp.bfloat16) for w in weights],
        bytes_accessed=10 << 20,
    )


def split_in(values, terms):
    parts = []
    for _ in range(terms):
        part = values.astype(jnp.bfloat16)
        parts.append(part)
        values = values - part.astype(jnp.float32)
    return parts


def stacked(*parts):
    rows = sum(part.shape[0] for part in parts)
    parts = [part.astype(jnp.float32) for part in parts]
    parts.append(jnp.zeros((-rows % 8, parts[0].shape[1]), jnp.float32))
    return jnp.concatenate(parts, axis=0).astype(jnp.bfloat16)


def prepare(step_bias, decay_log, skip_gain, inner, arrays, weights, rows_first):
    heads = step_bias.shape[1]
    head_dim = inner // heads
    count = 4 + len(arrays)
    wanted = [shaped(a.shape, a.dtype) for a in arrays]
    wanted.append(shaped((rows_first, weights.shape[1]), weights.dtype))

    def body(*refs):
        sources, (params_ref, spread_ref), outs = refs[:count], refs[count : count + 2], refs[count + 2 :]
        loaded, sems = outs[:-2], outs[-1]
        rows_ref = outs[-2]
        sources = [*sources[:-1], sources[-1].at[pl.ds(0, rows_first)]]
        targets = [rows_ref.at[pl.ds(i, 1)] for i in range(3)] + list(loaded)
        copies = [
            pltpu.make_async_copy(source, target, sems.at[i])
            for i, (source, target) in enumerate(zip(sources, targets))
        ]
        for copy in copies:
            copy.start()
        head = lax.broadcasted_iota(jnp.int32, (heads, inner), 0) * head_dim
        channel = lax.broadcasted_iota(jnp.int32, (heads, inner), 1)
        inside = (channel >= head) & (channel < head + head_dim)
        spread = jnp.where(inside, 1.0, 0.0).astype(jnp.bfloat16)
        spread_ref[...] = spread
        for copy in copies[:3]:
            copy.wait()
        rows = rows_ref[...]
        rows = jnp.concatenate([rows[0:1], jnp.exp(rows[1:2]), rows[2:3]], axis=0)
        total = jnp.zeros((3, inner), jnp.float32)
        for part in reversed(split_in(rows, 3)):
            total += jnp.dot(part, spread, preferred_element_type=jnp.float32)
        params_ref[...] = total
        for copy in copies[3:]:
            copy.wait()

    params, spread, *loaded = local_kernel(
        body,
        "prepare",
        [shaped((3, inner)), shaped((heads, inner), jnp.bfloat16)]
        + wanted,
        [(a, IN_HBM) for a in (step_bias, decay_log, skip_gain, *arrays, weights)],
        [pltpu.VMEM((3, heads), jnp.float32), pltpu.SemaphoreType.DMA((count,))],
        bytes_accessed=4 << 20,
    )
    return params, spread, loaded


def mix(parts, head_params, spread, convs, windows, norm_gain, ssm_state, steps):
    own_rows, heads, head_dim, state_size = ssm_state.shape
    block, columns = parts[0].shape
    inner, width = convs[0].shape[1], convs[1].shape[1]
    groups = width // state_size
    heads_group = heads // groups
    channels = heads_group * head_dim
    taps = convs[0].shape[0]
    count = len(parts)
    edges = (0, inner, 2 * inner, 2 * inner + width, 2 * inner + 2 * width, columns)
    terms = 1 + steps

    def body(*refs):
        part_refs = refs[:count]
        params_ref, spread_ref, *rest = refs[count:]
        conv_refs, window_refs = rest[:3], rest[3:6]
        gain_ref, state_ref, normed_ref, pre_ref, coef_ref, write_ref = rest[6:]
        total = part_refs[0][...]
        for ref in part_refs[1:]:
            total = total + ref[...].astype(jnp.float32)
        rounded = total.astype(jnp.bfloat16).astype(jnp.float32)
        pre_ref[...] = rounded[:, edges[1] : edges[4]]
        gate, *newest = [rounded[:, edges[i] : edges[i + 1]] for i in range(4)]
        bias, rate, skip = [params_ref[i : i + 1] for i in range(3)]
        step_pre = jnp.dot(
            rounded[:, edges[4] :].astype(jnp.bfloat16),
            spread_ref[...],
            preferred_element_type=jnp.float32,
        )
        step_size = jax.nn.softplus(step_pre + bias)
        decay = jnp.exp(-step_size * rate)
        gate = silu_float(gate)
        normed = []
        for own in range(own_rows):
            mine = slice(own * steps, (own + 1) * steps)
            acts = []
            for which in range(3):
                taps_in = conv_refs[which][...]
                earlier = window_refs[which][own].astype(jnp.float32)
                line = jnp.concatenate([earlier, newest[which][mine]], axis=0)
                acts.append(
                    silu_float(
                        added([line[k : k + steps] * taps_in[k : k + 1] for k in range(taps)])
                    )
                )
            input_act, write_act, read_act = acts
            write_ref[pl.ds(own * steps, steps), :] = write_act
            decays = decay[mine]
            fresh = step_size[mine] * input_act
            coefs = [fresh[s : s + 1] for s in range(steps)]
            kept = jnp.ones_like(decays[0:1])
            for s in reversed(range(steps)):
                coefs[s] = coefs[s] * kept
                kept = kept * decays[s : s + 1]
            coef_ref[own] = jnp.concatenate([kept] + coefs, axis=0)
            normed.append([])
            for g in range(groups):
                span = slice(g * channels, (g + 1) * channels)
                lanes = slice(g * state_size, (g + 1) * state_size)
                state = state_ref[own, g * heads_group : (g + 1) * heads_group]
                state = state.reshape(channels, state_size)
                high, low = [p.astype(jnp.float32) for p in split_in(read_act[:, lanes], 2)]
                reads = jnp.concatenate([high, low], axis=0).astype(jnp.bfloat16)
                by_high, by_low = [
                    lax.dot_general(
                        reads, p, (((1,), (1,)), ((), ())), preferred_element_type=jnp.float32
                    )
                    for p in split_in(state, 2)
                ]
                product = by_high[:steps] + by_high[steps:] + by_low[:steps]
                values = []
                for s in range(steps):
                    value = product[s : s + 1]
                    for j in range(s + 1):
                        overlap = jnp.sum(
                            write_act[j : j + 1, lanes] * read_act[s : s + 1, lanes],
                            axis=1,
                            keepdims=True,
                        )
                        value = decays[j : j + 1, span] * value + fresh[j : j + 1, span] * overlap
                    values.append(value)
                value = jnp.concatenate(values, axis=0) + skip[:, span] * input_act[:, span]
                value = value * gate[mine, span]
                mean = jnp.mean(value * value, axis=1, keepdims=True)
                normed[own].append(value * lax.rsqrt(mean + 1e-05) * gain_ref[:, span])
        normed = [jnp.concatenate(row, axis=1) for row in normed]
        normed_ref[...] = jnp.concatenate(normed, axis=0).astype(jnp.bfloat16)

    return local_kernel(
        body,
        "mix",
        [
            shaped((block, inner), jnp.bfloat16),
            shaped((block, inner + 2 * width)),
            shaped((own_rows, terms, inner)),
            shaped((block, width)),
        ],
        [(a, IN_VMEM) for a in (*parts, head_params, spread, *convs, *windows, norm_gain, ssm_state)],
        bytes_accessed=4 << 20,
    )


def renew(pre, coefs, writes, windows, ssm_state, tokens):
    steps, rows_all, depth = tokens.shape
    own_rows, heads, head_dim, state_size = ssm_state.shape
    groups = writes.shape[1] // state_size
    heads_group = heads // groups
    inner = coefs.shape[2]
    widths = [w.shape[2] for w in windows]

    def body(pre_ref, coef_ref, write_ref, *rest):
        window_refs, (state_ref, tokens_ref, final_ref, current_ref) = rest[:3], rest[3:7]
        out_refs = rest[7:]
        for s in range(steps):
            current_ref[pl.ds(s * rows_all, rows_all), :] = tokens_ref[s].astype(jnp.float32)
        for own in range(own_rows):
            first = own * steps
            base = 0
            for window_ref, out_ref, width in zip(window_refs, out_refs, widths):
                line = jnp.concatenate(
                    [
                        window_ref[own].astype(jnp.float32),
                        pre_ref[pl.ds(first, steps), pl.ds(base, width)],
                    ],
                    axis=0,
                )
                out_ref[own] = line[steps:].astype(jnp.bfloat16)
                base += width
            coefs_high, coefs_low = split_in(coef_ref[own, 1 : 1 + steps, :], 2)
            writes_high, writes_low = split_in(write_ref[pl.ds(first, steps), :], 2)
            left = stacked(coefs_high, coefs_high, coefs_low)
            right = stacked(writes_high, writes_low, writes_high)
            for g in range(groups):
                fresh = lax.dot_general(
                    left[:, g * heads_group * head_dim : (g + 1) * heads_group * head_dim],
                    right[:, g * state_size : (g + 1) * state_size],
                    (((0,), (0,)), ((), ())),
                    preferred_element_type=jnp.float32,
                )
                for i in range(heads_group):
                    h = g * heads_group + i
                    kept = coef_ref[own, 0:1, pl.ds(h * head_dim, 1)]
                    final_ref[own, h] = (
                        kept * state_ref[own, h] + fresh[i * head_dim : (i + 1) * head_dim]
                    )

    return local_kernel(
        body,
        "renew",
        [shaped(ssm_state.shape), shaped((steps * rows_all, depth))]
        + [shaped(w.shape, jnp.bfloat16) for w in windows],
        [(a, IN_VMEM) for a in (pre, coefs, writes, *windows, ssm_state, tokens)],
        bytes_accessed=4 << 20,
    )


def fetch(array, start, after):
    rows = array.shape[0] - start

    def body(source, _, target, sem):
        copy = pltpu.make_async_copy(source.at[pl.ds(start, rows)], target, sem)
        copy.start()
        copy.wait()

    return local_kernel(
        body,
        "fetch",
        shaped((rows, array.shape[1]), array.dtype),
        [(array, IN_HBM), (after, IN_VMEM)],
        [pltpu.SemaphoreType.DMA],
        bytes_accessed=8 << 20,
    )


def project_out(normed, parts, steps):
    owners = len(normed)
    block, inner = normed[0].shape
    own_rows = block // steps
    rows = own_rows * owners

    def body(*refs):
        out_ref, sent_ref, lhs = refs[owners + len(parts) :]
        for slot in range(owners):
            owner = owner_of(slot, "expert")
            values = refs[slot][...].astype(jnp.float32)
            for own in range(own_rows):
                for s in range(steps):
                    row = s * rows + owner * own_rows + own
                    lhs[pl.ds(row, 1), :] = values[own * steps + s : own * steps + s + 1]
        products = []
        base = 0
        for ref in refs[owners : owners + len(parts)]:
            values = lhs[:, pl.ds(base, ref.shape[0])].astype(jnp.bfloat16)
            products.append(jnp.dot(values, ref[...], preferred_element_type=jnp.float32))
            base += ref.shape[0]
        total = added(products)
        out_ref[...] = total
        sent_ref[...] = total.astype(jnp.bfloat16)

    return local_kernel(
        body,
        "project_out",
        sent_narrow((rows * steps, parts[0].shape[1]), 2),
        [(a, IN_VMEM) for a in (*normed, *parts)],
        [pltpu.VMEM((rows * steps, inner), jnp.float32)],
        bytes_accessed=4 << 20,
    )


def slot_rows(slot, width):
    start = owner_of(slot, "expert") * width
    return pl.ds(pl.multiple_of(start, width) if pairwise("expert") else start, width)


def expert_near(moe_in, expert_up):
    count = len(moe_in)
    many, width = moe_in[0].shape
    local_experts, _, hidden_width = expert_up.shape

    def body(*refs):
        up_ref, out_ref = refs[count:]
        for e in range(local_experts):
            out_ref[e] = added(
                [
                    jnp.dot(
                        refs[slot][...],
                        up_ref[e, slot_rows(slot, width), :],
                        preferred_element_type=jnp.float32,
                    )
                    for slot in range(count)
                ]
            )

    return local_kernel(
        body,
        "expert_near",
        shaped((local_experts, many, hidden_width)),
        [(a, IN_VMEM) for a in (*moe_in, expert_up)],
        bytes_accessed=4 << 20,
    )


def row_weights(chosen_ref, gates_ref, local_experts):
    first = lax.axis_index("expert") * local_experts
    steps = chosen_ref.shape[0]
    return [
        jnp.concatenate(
            [
                jnp.sum(
                    jnp.where(chosen_ref[s] == first + e, gates_ref[s], 0.0),
                    axis=1,
                    keepdims=True,
                )
                for s in range(steps)
            ],
            axis=0,
        )
        for e in range(local_experts)
    ]


def gated_sum(hidden_ref, weights, down_ref, columns):
    return added(
        [
            weights[e]
            * jnp.dot(
                hidden_ref[e], down_ref[e, :, columns], preferred_element_type=jnp.float32
            )
            for e in range(len(weights))
        ]
    )


def experts_far(near, moe_in, chosen, gates, expert_up, expert_down, owners):
    count = len(moe_in)
    many, width = moe_in[0].shape
    local_experts, _, hidden_width = expert_up.shape
    far = range(1, owners)

    def body(*refs):
        near_ref, chosen_ref, gates_ref, up_ref, down_ref, hidden_ref, *outs = refs[count:]
        for e in range(local_experts):
            total = near_ref[e]
            for i in range(count):
                total += jnp.dot(
                    refs[i][...],
                    up_ref[e, slot_rows(owners - count + i, width), :],
                    preferred_element_type=jnp.float32,
                )
            total = jnp.maximum(total, 0.0)
            hidden_ref[e] = (total * total).astype(jnp.bfloat16)
        weights = row_weights(chosen_ref, gates_ref, local_experts)
        for slot, out in zip(far, outs):
            total = gated_sum(hidden_ref, weights, down_ref, slot_rows(slot, width))
            out[...] = total.astype(out.dtype)

    hidden, *outs = local_kernel(
        body,
        "experts_far",
        [shaped((local_experts, many, hidden_width), jnp.bfloat16)]
        + sent_narrow((many, width), 1 + len(far))[1:],
        [(a, IN_VMEM) for a in (*moe_in, near, chosen, gates, expert_up, expert_down)],
        bytes_accessed=16 << 20,
    )
    return hidden, outs


def experts_close(hidden, chosen, gates, expert_down, owners):
    local_experts, many, _ = hidden.shape
    width = expert_down.shape[2] // owners

    def body(hidden_ref, chosen_ref, gates_ref, down_ref, *outs):
        weights = row_weights(chosen_ref, gates_ref, local_experts)
        for slot, out in enumerate(outs):
            total = gated_sum(hidden_ref, weights, down_ref, slot_rows(slot, width))
            out[...] = total.astype(out.dtype)

    return local_kernel(
        body,
        "experts_close",
        sent_narrow((many, width), 1),
        [(a, IN_VMEM) for a in (hidden, chosen, gates, expert_down)],
        bytes_accessed=4 << 20,
    )


def finish(parts, shape):
    steps, rows, _ = shape

    def body(*refs):
        total = added([ref[...] for ref in refs[:-1]])
        for s in range(steps):
            refs[-1][s] = total[s * rows : (s + 1) * rows].astype(jnp.bfloat16)

    return local_kernel(body, "finish", shaped(shape, jnp.bfloat16), [(p, IN_VMEM) for p in parts])


def per_device(
    tokens,
    proj_gate,
    proj_input,
    proj_write,
    proj_read,
    proj_step,
    conv_input,
    conv_write,
    conv_read,
    window_input,
    window_write,
    window_read,
    step_bias,
    decay_log,
    skip_gain,
    norm_gain,
    ssm_state,
    out_proj,
    expert_up,
    expert_down,
    expert_ids,
    route_gates,
):
    steps = tokens.shape[0]
    inner = conv_input.shape[1]
    windows = (window_input, window_write, window_read)
    projected = project(
        lax.axis_size("expert"),
        tokens,
        (proj_gate, proj_input, proj_write, proj_read),
        proj_step.T,
    )
    head_params, spread, loaded = prepare(
        *[p.reshape(1, -1) for p in (step_bias, decay_log, skip_gain)],
        inner,
        (conv_input, conv_write, conv_read, *windows, norm_gain.reshape(1, -1), ssm_state)
        + (tokens, expert_ids, route_gates),
        out_proj,
        inner // FIRST,
    )
    convs, windows = loaded[:3], loaded[3:6]
    norm_gain, ssm_state, tokens, expert_ids, route_gates, out_first = loaded[6:]
    normed, pre, coefs, writes = mix(
        scatter_parts(projected, "expert"),
        head_params,
        spread,
        convs,
        windows,
        norm_gain,
        ssm_state,
        steps,
    )
    partial, sent = project_out(gather(normed, "expert"), (out_first, fetch(out_proj, inner // FIRST, writes)), steps)
    ssm_final, current, *finals = renew(pre, coefs, writes, windows, ssm_state, tokens)
    residual = added([current] + sum_parts(partial, "tensor", sent, ((2, 0, 3, 1), (3, 2, 1, 0), (1, 3, 0, 2))))
    moe_in = gather(residual.astype(jnp.bfloat16), "expert")
    expert_up, expert_down = resident(expert_up), resident(expert_down)
    near = expert_near(moe_in[:NEAR], expert_up)
    owners = len(moe_in)
    hidden, far = experts_far(
        near, moe_in[NEAR:], expert_ids, route_gates, expert_up, expert_down, owners
    )
    moe_sum = [*experts_close(hidden, expert_ids, route_gates, expert_down, owners), *far]
    moe_sum = added(scatter_parts(moe_sum, "expert"))
    mixed_out = finish([residual] + sum_parts(moe_sum, "tensor", moe_sum.astype(jnp.bfloat16), ((1, 0, 3, 2), (2, 3, 0, 1), (3, 2, 1, 0))), tokens.shape)
    return (mixed_out, ssm_final, *finals)


def solution(mesh):
    placed = (
        P(None, "groups", "expert"),
        P("expert", "tensor"),
        P("expert", "tensor"),
        P("expert", "tensor"),
        P("expert", "tensor"),
        P("expert", "tensor"),
        P(None, "tensor"),
        P(None, "tensor"),
        P(None, "tensor"),
        P(("groups", "expert"), None, "tensor"),
        P(("groups", "expert"), None, "tensor"),
        P(("groups", "expert"), None, "tensor"),
        P("tensor"),
        P("tensor"),
        P("tensor"),
        P("tensor"),
        P(("groups", "expert"), "tensor", None, None),
        P("tensor", "expert"),
        P("expert", None, "tensor"),
        P("expert", "tensor", None),
        P(None, "groups", None),
        P(None, "groups", None),
    )
    return jax.shard_map(
        per_device,
        mesh=mesh,
        in_specs=placed,
        out_specs=(
            P(None, "groups", "expert"),
            P(("groups", "expert"), "tensor", None, None),
            P(("groups", "expert"), None, "tensor"),
            P(("groups", "expert"), None, "tensor"),
            P(("groups", "expert"), None, "tensor"),
        ),
        check_vma=False,
    )
```

```python
import jax
import jax.numpy as jnp
from jax import lax
from jax.experimental import pallas as pl
from jax.experimental.pallas import tpu as pltpu
from jax.sharding import PartitionSpec as P


def silu_float(values):
    return values / (1.0 + jnp.exp(-values))


def pairwise(axis):
    size = lax.axis_size(axis)
    return size <= 4 and size & (size - 1) == 0


def swap(values, axis, distance):
    size = lax.axis_size(axis)
    return lax.ppermute(values, axis, [(i, i ^ distance) for i in range(size)])


def gather(values, axis):
    size = lax.axis_size(axis)
    if not pairwise(axis):
        held = lax.all_gather(values, axis, axis=0)
        return [held[j] for j in range(size)]
    return [values] + [swap(values, axis, d) for d in range(1, size)]


def sum_parts(values, axis, sent, order):
    if not pairwise(axis):
        return [lax.psum(values, axis)]
    if lax.axis_size(axis) != 4:
        return [values] + [swap(sent, axis, d) for d in range(1, lax.axis_size(axis))]
    return [values] + [lax.ppermute(sent, axis, list(enumerate(p))) for p in order]


def scatter_parts(blocks, axis):
    if not pairwise(axis):
        blocks = jnp.stack([block.astype(jnp.float32) for block in blocks])
        return [lax.psum_scatter(blocks, axis, scatter_dimension=0, tiled=False)]
    return [blocks[0]] + [swap(blocks[d], axis, d) for d in (2, 3, 1) if d < len(blocks)]


def added(parts):
    total = parts[0]
    for part in parts[1:]:
        total = total + part.astype(total.dtype)
    return total


def owner_of(slot, axis):
    return lax.axis_index(axis) ^ slot if pairwise(axis) else slot


VMEM_LIMIT = 16 * 1024 * 1024
IN_VMEM = pl.BlockSpec(memory_space=pltpu.VMEM)
IN_HBM = pl.BlockSpec(memory_space=pltpu.HBM)
CHUNK = 512 * 1024
FIRST = 4
NEAR = 1


def local_kernel(body, name, out_shape, ins, scratch=(), bytes_accessed=1 << 20):
    return pl.pallas_call(
        body,
        out_shape=out_shape,
        in_specs=[spec for _, spec in ins],
        out_specs=jax.tree.map(lambda _: IN_VMEM, out_shape),
        scratch_shapes=list(scratch),
        compiler_params=pltpu.CompilerParams(vmem_limit_bytes=VMEM_LIMIT),
        cost_estimate=pl.CostEstimate(
            flops=bytes_accessed, bytes_accessed=bytes_accessed, transcendentals=0
        ),
        name=name,
    )(*[held(array, spec) for array, spec in ins])


def held(array, spec):
    if spec is IN_HBM:
        return pltpu.with_memory_space_constraint(array, pltpu.HBM)
    return array


def resident(array):
    return pltpu.with_memory_space_constraint(array, pltpu.VMEM)


def shaped(shape, dtype=jnp.float32):
    return jax.ShapeDtypeStruct(tuple(shape), dtype)


def kept_and_sent(shape, slots):
    return [shaped(shape)] * slots


def project(owners, tokens, weights, step_weights):
    steps, rows, depth = tokens.shape
    own_rows = rows // owners
    widths = [w.shape[1] for w in weights]
    heads = step_weights.shape[0]
    columns = sum(widths) + heads
    block = own_rows * steps
    pieces = []
    for index, width in enumerate(widths):
        size = max(16, min(depth, CHUNK // width))
        pieces += [(index, start, min(size, depth - start)) for start in range(0, depth, size)]
    bases = [sum(widths[:index]) for index in range(len(widths))]
    count = len(weights)

    def body(*refs):
        tokens_ref, step_ref = refs[:2]
        weight_refs = refs[2 : 2 + count]
        outs = refs[2 + count : 2 + count + owners]
        tokens_in, step_in, wide, lhs, sems, *weights_in = refs[2 + count + owners :]
        first = [
            pltpu.make_async_copy(tokens_ref, tokens_in, sems.at[0]),
            pltpu.make_async_copy(step_ref, step_in, sems.at[1]),
        ]
        copies = [
            pltpu.make_async_copy(
                weight_refs[index].at[pl.ds(start, size)],
                weights_in[index].at[pl.ds(start, size)],
                sems.at[2 + i],
            )
            for i, (index, start, size) in enumerate(pieces)
        ]
        for copy in first + copies:
            copy.start()
        first[0].wait()
        wide[...] = tokens_in[...].astype(jnp.float32)
        for slot in range(owners):
            owner = owner_of(slot, "expert")
            for own in range(own_rows):
                for s in range(steps):
                    row = slot * block + own * steps + s
                    lhs[pl.ds(row, 1), :] = wide[s, pl.ds(owner * own_rows + own, 1), :]
        rows_in = lhs[...].astype(jnp.bfloat16)

        def put(place, size, result):
            for slot in range(owners):
                part = result[slot * block : (slot + 1) * block]
                outs[slot][:, pl.ds(place, size)] = part.astype(outs[slot].dtype)

        first[1].wait()
        put(
            columns - heads,
            heads,
            lax.dot_general(
                rows_in,
                step_in[...],
                (((1,), (1,)), ((), ())),
                preferred_element_type=jnp.float32,
            ),
        )
        total = None
        for copy, (index, start, size) in zip(copies, pieces):
            copy.wait()
            product = jnp.dot(
                rows_in[:, start : start + size],
                weights_in[index][pl.ds(start, size)],
                preferred_element_type=jnp.float32,
            )
            total = product if start == 0 else total + product
            if start + size == depth:
                put(bases[index], widths[index], total)

    return local_kernel(
        body,
        "project",
        kept_and_sent((block, columns), owners),
        [(tokens, IN_HBM), (step_weights, IN_HBM)] + [(w, IN_HBM) for w in weights],
        [
            pltpu.VMEM(tokens.shape, jnp.bfloat16),
            pltpu.VMEM(step_weights.shape, jnp.bfloat16),
            pltpu.VMEM(tokens.shape, jnp.float32),
            pltpu.VMEM((owners * block, depth), jnp.float32),
            pltpu.SemaphoreType.DMA((2 + len(pieces),)),
        ]
        + [pltpu.VMEM(w.shape, jnp.bfloat16) for w in weights],
        bytes_accessed=10 << 20,
    )


def split_in(values, terms):
    parts = []
    for _ in range(terms):
        part = values.astype(jnp.bfloat16)
        parts.append(part)
        values = values - part.astype(jnp.float32)
    return parts


def stacked(*parts):
    rows = sum(part.shape[0] for part in parts)
    parts = [part.astype(jnp.float32) for part in parts]
    parts.append(jnp.zeros((-rows % 8, parts[0].shape[1]), jnp.float32))
    return jnp.concatenate(parts, axis=0).astype(jnp.bfloat16)


def prepare(step_bias, decay_log, skip_gain, inner, arrays, weights, rows_first):
    heads = step_bias.shape[1]
    head_dim = inner // heads
    count = 4 + len(arrays)
    wanted = [shaped(a.shape, a.dtype) for a in arrays]
    wanted.append(shaped((rows_first, weights.shape[1]), weights.dtype))

    def body(*refs):
        sources, (params_ref, spread_ref), outs = refs[:count], refs[count : count + 2], refs[count + 2 :]
        loaded, sems = outs[:-2], outs[-1]
        rows_ref = outs[-2]
        sources = [*sources[:-1], sources[-1].at[pl.ds(0, rows_first)]]
        targets = [rows_ref.at[pl.ds(i, 1)] for i in range(3)] + list(loaded)
        copies = [
            pltpu.make_async_copy(source, target, sems.at[i])
            for i, (source, target) in enumerate(zip(sources, targets))
        ]
        for copy in copies:
            copy.start()
        head = lax.broadcasted_iota(jnp.int32, (heads, inner), 0) * head_dim
        channel = lax.broadcasted_iota(jnp.int32, (heads, inner), 1)
        inside = (channel >= head) & (channel < head + head_dim)
        spread = jnp.where(inside, 1.0, 0.0).astype(jnp.bfloat16)
        spread_ref[...] = spread
        for copy in copies[:3]:
            copy.wait()
        rows = rows_ref[...]
        rows = jnp.concatenate([rows[0:1], jnp.exp(rows[1:2]), rows[2:3]], axis=0)
        total = jnp.zeros((3, inner), jnp.float32)
        for part in reversed(split_in(rows, 3)):
            total += jnp.dot(part, spread, preferred_element_type=jnp.float32)
        params_ref[...] = total
        for copy in copies[3:]:
            copy.wait()

    params, spread, *loaded = local_kernel(
        body,
        "prepare",
        [shaped((3, inner)), shaped((heads, inner), jnp.bfloat16)]
        + wanted,
        [(a, IN_HBM) for a in (step_bias, decay_log, skip_gain, *arrays, weights)],
        [pltpu.VMEM((3, heads), jnp.float32), pltpu.SemaphoreType.DMA((count,))],
        bytes_accessed=4 << 20,
    )
    return params, spread, loaded


def mix(parts, head_params, spread, convs, windows, norm_gain, ssm_state, steps):
    own_rows, heads, head_dim, state_size = ssm_state.shape
    block, columns = parts[0].shape
    inner, width = convs[0].shape[1], convs[1].shape[1]
    groups = width // state_size
    heads_group = heads // groups
    channels = heads_group * head_dim
    taps = convs[0].shape[0]
    count = len(parts)
    edges = (0, inner, 2 * inner, 2 * inner + width, 2 * inner + 2 * width, columns)
    terms = 1 + steps

    def body(*refs):
        part_refs = refs[:count]
        params_ref, spread_ref, *rest = refs[count:]
        conv_refs, window_refs = rest[:3], rest[3:6]
        gain_ref, state_ref, normed_ref, pre_ref, coef_ref, write_ref = rest[6:]
        total = part_refs[0][...]
        for ref in part_refs[1:]:
            total = total + ref[...].astype(jnp.float32)
        rounded = total.astype(jnp.bfloat16).astype(jnp.float32)
        pre_ref[...] = rounded[:, edges[1] : edges[4]]
        gate, *newest = [rounded[:, edges[i] : edges[i + 1]] for i in range(4)]
        bias, rate, skip = [params_ref[i : i + 1] for i in range(3)]
        step_pre = jnp.dot(
            rounded[:, edges[4] :].astype(jnp.bfloat16),
            spread_ref[...],
            preferred_element_type=jnp.float32,
        )
        step_size = jax.nn.softplus(step_pre + bias)
        decay = jnp.exp(-step_size * rate)
        gate = silu_float(gate)
        normed = []
        for own in range(own_rows):
            mine = slice(own * steps, (own + 1) * steps)
            acts = []
            for which in range(3):
                taps_in = conv_refs[which][...]
                earlier = window_refs[which][own].astype(jnp.float32)
                line = jnp.concatenate([earlier, newest[which][mine]], axis=0)
                acts.append(
                    silu_float(
                        added([line[k : k + steps] * taps_in[k : k + 1] for k in range(taps)])
                    )
                )
            input_act, write_act, read_act = acts
            write_ref[pl.ds(own * steps, steps), :] = write_act
            decays = decay[mine]
            fresh = step_size[mine] * input_act
            coefs = [fresh[s : s + 1] for s in range(steps)]
            kept = jnp.ones_like(decays[0:1])
            for s in reversed(range(steps)):
                coefs[s] = coefs[s] * kept
                kept = kept * decays[s : s + 1]
            coef_ref[own] = jnp.concatenate([kept] + coefs, axis=0)
            normed.append([])
            for g in range(groups):
                span = slice(g * channels, (g + 1) * channels)
                lanes = slice(g * state_size, (g + 1) * state_size)
                state = state_ref[own, g * heads_group : (g + 1) * heads_group]
                state = state.reshape(channels, state_size)
                high, low = [p.astype(jnp.float32) for p in split_in(read_act[:, lanes], 2)]
                reads = jnp.concatenate([high, low], axis=0).astype(jnp.bfloat16)
                by_high, by_low = [
                    lax.dot_general(
                        reads, p, (((1,), (1,)), ((), ())), preferred_element_type=jnp.float32
                    )
                    for p in split_in(state, 2)
                ]
                product = by_high[:steps] + by_high[steps:] + by_low[:steps]
                values = []
                for s in range(steps):
                    value = product[s : s + 1]
                    for j in range(s + 1):
                        overlap = jnp.sum(
                            write_act[j : j + 1, lanes] * read_act[s : s + 1, lanes],
                            axis=1,
                            keepdims=True,
                        )
                        value = decays[j : j + 1, span] * value + fresh[j : j + 1, span] * overlap
                    values.append(value)
                value = jnp.concatenate(values, axis=0) + skip[:, span] * input_act[:, span]
                value = value * gate[mine, span]
                mean = jnp.mean(value * value, axis=1, keepdims=True)
                normed[own].append(value * lax.rsqrt(mean + 1e-05) * gain_ref[:, span])
        normed = [jnp.concatenate(row, axis=1) for row in normed]
        normed_ref[...] = jnp.concatenate(normed, axis=0).astype(jnp.bfloat16)

    return local_kernel(
        body,
        "mix",
        [
            shaped((block, inner), jnp.bfloat16),
            shaped((block, inner + 2 * width)),
            shaped((own_rows, terms, inner)),
            shaped((block, width)),
        ],
        [(a, IN_VMEM) for a in (*parts, head_params, spread, *convs, *windows, norm_gain, ssm_state)],
        bytes_accessed=4 << 20,
    )


def renew(pre, coefs, writes, windows, ssm_state, tokens):
    steps, rows_all, depth = tokens.shape
    own_rows, heads, head_dim, state_size = ssm_state.shape
    groups = writes.shape[1] // state_size
    heads_group = heads // groups
    inner = coefs.shape[2]
    widths = [w.shape[2] for w in windows]

    def body(pre_ref, coef_ref, write_ref, *rest):
        window_refs, (state_ref, tokens_ref, final_ref, current_ref) = rest[:3], rest[3:7]
        out_refs = rest[7:]
        for s in range(steps):
            current_ref[pl.ds(s * rows_all, rows_all), :] = tokens_ref[s].astype(jnp.float32)
        for own in range(own_rows):
            first = own * steps
            base = 0
            for window_ref, out_ref, width in zip(window_refs, out_refs, widths):
                line = jnp.concatenate(
                    [
                        window_ref[own].astype(jnp.float32),
                        pre_ref[pl.ds(first, steps), pl.ds(base, width)],
                    ],
                    axis=0,
                )
                out_ref[own] = line[steps:].astype(jnp.bfloat16)
                base += width
            coefs_high, coefs_low = split_in(coef_ref[own, 1 : 1 + steps, :], 2)
            writes_high, writes_low = split_in(write_ref[pl.ds(first, steps), :], 2)
            left = stacked(coefs_high, coefs_high, coefs_low)
            right = stacked(writes_high, writes_low, writes_high)
            for g in range(groups):
                fresh = lax.dot_general(
                    left[:, g * heads_group * head_dim : (g + 1) * heads_group * head_dim],
                    right[:, g * state_size : (g + 1) * state_size],
                    (((0,), (0,)), ((), ())),
                    preferred_element_type=jnp.float32,
                )
                for i in range(heads_group):
                    h = g * heads_group + i
                    kept = coef_ref[own, 0:1, pl.ds(h * head_dim, 1)]
                    final_ref[own, h] = (
                        kept * state_ref[own, h] + fresh[i * head_dim : (i + 1) * head_dim]
                    )

    return local_kernel(
        body,
        "renew",
        [shaped(ssm_state.shape), shaped((steps * rows_all, depth))]
        + [shaped(w.shape, jnp.bfloat16) for w in windows],
        [(a, IN_VMEM) for a in (pre, coefs, writes, *windows, ssm_state, tokens)],
        bytes_accessed=4 << 20,
    )


def fetch(array, start, after):
    rows = array.shape[0] - start

    def body(source, _, target, sem):
        copy = pltpu.make_async_copy(source.at[pl.ds(start, rows)], target, sem)
        copy.start()
        copy.wait()

    return local_kernel(
        body,
        "fetch",
        shaped((rows, array.shape[1]), array.dtype),
        [(array, IN_HBM), (after, IN_VMEM)],
        [pltpu.SemaphoreType.DMA],
        bytes_accessed=8 << 20,
    )


def project_out(normed, parts, steps):
    owners = len(normed)
    block, inner = normed[0].shape
    own_rows = block // steps
    rows = own_rows * owners

    def body(*refs):
        out_ref, sent_ref, lhs = refs[owners + len(parts) :]
        for slot in range(owners):
            owner = owner_of(slot, "expert")
            values = refs[slot][...].astype(jnp.float32)
            for own in range(own_rows):
                for s in range(steps):
                    row = s * rows + owner * own_rows + own
                    lhs[pl.ds(row, 1), :] = values[own * steps + s : own * steps + s + 1]
        products = []
        base = 0
        for ref in refs[owners : owners + len(parts)]:
            values = lhs[:, pl.ds(base, ref.shape[0])].astype(jnp.bfloat16)
            products.append(jnp.dot(values, ref[...], preferred_element_type=jnp.float32))
            base += ref.shape[0]
        total = added(products)
        out_ref[...] = total
        sent_ref[...] = total.astype(sent_ref.dtype)

    return local_kernel(
        body,
        "project_out",
        kept_and_sent((rows * steps, parts[0].shape[1]), 2),
        [(a, IN_VMEM) for a in (*normed, *parts)],
        [pltpu.VMEM((rows * steps, inner), jnp.float32)],
        bytes_accessed=4 << 20,
    )


def slot_rows(slot, width):
    start = owner_of(slot, "expert") * width
    return pl.ds(pl.multiple_of(start, width) if pairwise("expert") else start, width)


def expert_near(moe_in, expert_up):
    count = len(moe_in)
    many, width = moe_in[0].shape
    local_experts, _, hidden_width = expert_up.shape

    def body(*refs):
        up_ref, out_ref = refs[count:]
        for e in range(local_experts):
            out_ref[e] = added(
                [
                    jnp.dot(
                        refs[slot][...],
                        up_ref[e, slot_rows(slot, width), :],
                        preferred_element_type=jnp.float32,
                    )
                    for slot in range(count)
                ]
            )

    return local_kernel(
        body,
        "expert_near",
        shaped((local_experts, many, hidden_width)),
        [(a, IN_VMEM) for a in (*moe_in, expert_up)],
        bytes_accessed=4 << 20,
    )


def row_weights(chosen_ref, gates_ref, local_experts):
    first = lax.axis_index("expert") * local_experts
    steps = chosen_ref.shape[0]
    return [
        jnp.concatenate(
            [
                jnp.sum(
                    jnp.where(chosen_ref[s] == first + e, gates_ref[s], 0.0),
                    axis=1,
                    keepdims=True,
                )
                for s in range(steps)
            ],
            axis=0,
        )
        for e in range(local_experts)
    ]


def gated_sum(hidden_ref, weights, down_ref, columns):
    return added(
        [
            weights[e]
            * jnp.dot(
                hidden_ref[e], down_ref[e, :, columns], preferred_element_type=jnp.float32
            )
            for e in range(len(weights))
        ]
    )


def experts_far(near, moe_in, chosen, gates, expert_up, expert_down, owners):
    count = len(moe_in)
    many, width = moe_in[0].shape
    local_experts, _, hidden_width = expert_up.shape
    far = range(1, owners)

    def body(*refs):
        near_ref, chosen_ref, gates_ref, up_ref, down_ref, hidden_ref, *outs = refs[count:]
        for e in range(local_experts):
            total = near_ref[e]
            for i in range(count):
                total += jnp.dot(
                    refs[i][...],
                    up_ref[e, slot_rows(owners - count + i, width), :],
                    preferred_element_type=jnp.float32,
                )
            total = jnp.maximum(total, 0.0)
            hidden_ref[e] = (total * total).astype(jnp.bfloat16)
        weights = row_weights(chosen_ref, gates_ref, local_experts)
        for slot, out in zip(far, outs):
            total = gated_sum(hidden_ref, weights, down_ref, slot_rows(slot, width))
            out[...] = total.astype(out.dtype)

    hidden, *outs = local_kernel(
        body,
        "experts_far",
        [shaped((local_experts, many, hidden_width), jnp.bfloat16)]
        + kept_and_sent((many, width), 1 + len(far))[1:],
        [(a, IN_VMEM) for a in (*moe_in, near, chosen, gates, expert_up, expert_down)],
        bytes_accessed=16 << 20,
    )
    return hidden, outs


def experts_close(hidden, chosen, gates, expert_down, owners):
    local_experts, many, _ = hidden.shape
    width = expert_down.shape[2] // owners

    def body(hidden_ref, chosen_ref, gates_ref, down_ref, *outs):
        weights = row_weights(chosen_ref, gates_ref, local_experts)
        for slot, out in enumerate(outs):
            total = gated_sum(hidden_ref, weights, down_ref, slot_rows(slot, width))
            out[...] = total.astype(out.dtype)

    return local_kernel(
        body,
        "experts_close",
        kept_and_sent((many, width), 1),
        [(a, IN_VMEM) for a in (hidden, chosen, gates, expert_down)],
        bytes_accessed=4 << 20,
    )


def finish(parts, shape):
    steps, rows, _ = shape

    def body(*refs):
        total = added([ref[...] for ref in refs[:-1]])
        for s in range(steps):
            refs[-1][s] = total[s * rows : (s + 1) * rows].astype(jnp.bfloat16)

    return local_kernel(body, "finish", shaped(shape, jnp.bfloat16), [(p, IN_VMEM) for p in parts])


def per_device(
    tokens,
    proj_gate,
    proj_input,
    proj_write,
    proj_read,
    proj_step,
    conv_input,
    conv_write,
    conv_read,
    window_input,
    window_write,
    window_read,
    step_bias,
    decay_log,
    skip_gain,
    norm_gain,
    ssm_state,
    out_proj,
    expert_up,
    expert_down,
    expert_ids,
    route_gates,
):
    steps = tokens.shape[0]
    inner = conv_input.shape[1]
    windows = (window_input, window_write, window_read)
    projected = project(
        lax.axis_size("expert"),
        tokens,
        (proj_gate, proj_input, proj_write, proj_read),
        proj_step.T,
    )
    head_params, spread, loaded = prepare(
        *[p.reshape(1, -1) for p in (step_bias, decay_log, skip_gain)],
        inner,
        (conv_input, conv_write, conv_read, *windows, norm_gain.reshape(1, -1), ssm_state)
        + (tokens, expert_ids, route_gates),
        out_proj,
        inner // FIRST,
    )
    convs, windows = loaded[:3], loaded[3:6]
    norm_gain, ssm_state, tokens, expert_ids, route_gates, out_first = loaded[6:]
    normed, pre, coefs, writes = mix(
        scatter_parts(projected, "expert"),
        head_params,
        spread,
        convs,
        windows,
        norm_gain,
        ssm_state,
        steps,
    )
    partial, sent = project_out(gather(normed, "expert"), (out_first, fetch(out_proj, inner // FIRST, writes)), steps)
    ssm_final, current, *finals = renew(pre, coefs, writes, windows, ssm_state, tokens)
    residual = added([current] + sum_parts(partial, "tensor", sent, ((2, 0, 3, 1), (3, 2, 1, 0), (1, 3, 0, 2))))
    moe_in = gather(residual.astype(jnp.bfloat16), "expert")
    expert_up, expert_down = resident(expert_up), resident(expert_down)
    near = expert_near(moe_in[:NEAR], expert_up)
    owners = len(moe_in)
    hidden, far = experts_far(
        near, moe_in[NEAR:], expert_ids, route_gates, expert_up, expert_down, owners
    )
    moe_sum = [*experts_close(hidden, expert_ids, route_gates, expert_down, owners), *far]
    moe_sum = added(scatter_parts(moe_sum, "expert"))
    mixed_out = finish([residual] + sum_parts(moe_sum, "tensor", moe_sum, ((1, 0, 3, 2), (2, 3, 0, 1), (3, 2, 1, 0))), tokens.shape)
    return (mixed_out, ssm_final, *finals)


def solution(mesh):
    placed = (
        P(None, "groups", "expert"),
        P("expert", "tensor"),
        P("expert", "tensor"),
        P("expert", "tensor"),
        P("expert", "tensor"),
        P("expert", "tensor"),
        P(None, "tensor"),
        P(None, "tensor"),
        P(None, "tensor"),
        P(("groups", "expert"), None, "tensor"),
        P(("groups", "expert"), None, "tensor"),
        P(("groups", "expert"), None, "tensor"),
        P("tensor"),
        P("tensor"),
        P("tensor"),
        P("tensor"),
        P(("groups", "expert"), "tensor", None, None),
        P("tensor", "expert"),
        P("expert", None, "tensor"),
        P("expert", "tensor", None),
        P(None, "groups", None),
        P(None, "groups", None),
    )
    return jax.shard_map(
        per_device,
        mesh=mesh,
        in_specs=placed,
        out_specs=(
            P(None, "groups", "expert"),
            P(("groups", "expert"), "tensor", None, None),
            P(("groups", "expert"), None, "tensor"),
            P(("groups", "expert"), None, "tensor"),
            P(("groups", "expert"), None, "tensor"),
        ),
        check_vma=False,
    )
```

```python
import jax
import jax.numpy as jnp
from jax import lax
from jax.experimental import pallas as pl
from jax.experimental.pallas import tpu as pltpu
from jax.sharding import PartitionSpec as P


def silu_float(values):
    return values / (1.0 + jnp.exp(-values))


def pairwise(axis):
    size = lax.axis_size(axis)
    return size <= 4 and size & (size - 1) == 0


def swap(values, axis, distance):
    size = lax.axis_size(axis)
    return lax.ppermute(values, axis, [(i, i ^ distance) for i in range(size)])


def gather(values, axis):
    size = lax.axis_size(axis)
    if not pairwise(axis):
        held = lax.all_gather(values, axis, axis=0)
        return [held[j] for j in range(size)]
    return [values] + [swap(values, axis, d) for d in range(1, size)]


def sum_parts(values, axis, sent, order):
    if not pairwise(axis):
        return [lax.psum(values, axis)]
    if lax.axis_size(axis) != 4:
        return [values] + [swap(sent, axis, d) for d in range(1, lax.axis_size(axis))]
    return [values] + [lax.ppermute(sent, axis, list(enumerate(p))) for p in order]


def scatter_parts(blocks, axis):
    if not pairwise(axis):
        blocks = jnp.stack([block.astype(jnp.float32) for block in blocks])
        return [lax.psum_scatter(blocks, axis, scatter_dimension=0, tiled=False)]
    return [blocks[0]] + [swap(blocks[d], axis, d) for d in (2, 3, 1) if d < len(blocks)]


def added(parts):
    total = parts[0]
    for part in parts[1:]:
        total = total + part.astype(total.dtype)
    return total


def owner_of(slot, axis):
    return lax.axis_index(axis) ^ slot if pairwise(axis) else slot


VMEM_LIMIT = 16 * 1024 * 1024
IN_VMEM = pl.BlockSpec(memory_space=pltpu.VMEM)
IN_HBM = pl.BlockSpec(memory_space=pltpu.HBM)
CHUNK = 512 * 1024
COLUMNS = 512
FIRST = 4
NEAR = 1


def local_kernel(body, name, out_shape, ins, scratch=(), bytes_accessed=1 << 20):
    return pl.pallas_call(
        body,
        out_shape=out_shape,
        in_specs=[spec for _, spec in ins],
        out_specs=jax.tree.map(lambda _: IN_VMEM, out_shape),
        scratch_shapes=list(scratch),
        compiler_params=pltpu.CompilerParams(vmem_limit_bytes=VMEM_LIMIT),
        cost_estimate=pl.CostEstimate(
            flops=bytes_accessed, bytes_accessed=bytes_accessed, transcendentals=0
        ),
        name=name,
    )(*[held(array, spec) for array, spec in ins])


def held(array, spec):
    if spec is IN_HBM:
        return pltpu.with_memory_space_constraint(array, pltpu.HBM)
    return array


def resident(array):
    return pltpu.with_memory_space_constraint(array, pltpu.VMEM)


def shaped(shape, dtype=jnp.float32):
    return jax.ShapeDtypeStruct(tuple(shape), dtype)


def sent_narrow(shape, slots):
    return [shaped(shape)] + [shaped(shape, jnp.bfloat16)] * (slots - 1)


def project(owners, tokens, weights, step_weights):
    steps, rows, depth = tokens.shape
    own_rows = rows // owners
    widths = [w.shape[1] for w in weights]
    heads = step_weights.shape[0]
    columns = sum(widths) + heads
    block = own_rows * steps
    last = widths.index(max(widths), 1)
    pieces = []
    for index, width in enumerate(widths):
        size = max(16, min(depth, CHUNK // width))
        if index != last:
            pieces += [
                (index, start, min(size, depth - start), 0, width)
                for start in range(0, depth, size)
            ]
    pieces += [
        (last, 0, depth, start, min(COLUMNS, widths[last] - start))
        for start in range(0, widths[last], COLUMNS)
    ]
    bases = [sum(widths[:index]) for index in range(len(widths))]
    count = len(weights)

    def body(*refs):
        tokens_ref, step_ref = refs[:2]
        weight_refs = refs[2 : 2 + count]
        outs = refs[2 + count : 2 + count + owners]
        tokens_in, step_in, wide, lhs, sems, *weights_in = refs[2 + count + owners :]
        first = [
            pltpu.make_async_copy(tokens_ref, tokens_in, sems.at[0]),
            pltpu.make_async_copy(step_ref, step_in, sems.at[1]),
        ]
        copies = [
            pltpu.make_async_copy(
                weight_refs[index].at[pl.ds(start, size), pl.ds(left, wide_by)],
                weights_in[index].at[pl.ds(start, size), pl.ds(left, wide_by)],
                sems.at[2 + i],
            )
            for i, (index, start, size, left, wide_by) in enumerate(pieces)
        ]
        for copy in first + copies:
            copy.start()
        first[0].wait()
        wide[...] = tokens_in[...].astype(jnp.float32)
        for slot in range(owners):
            owner = owner_of(slot, "expert")
            for own in range(own_rows):
                for s in range(steps):
                    row = slot * block + own * steps + s
                    lhs[pl.ds(row, 1), :] = wide[s, pl.ds(owner * own_rows + own, 1), :]
        rows_in = lhs[...].astype(jnp.bfloat16)

        def put(place, size, result):
            for slot in range(owners):
                part = result[slot * block : (slot + 1) * block]
                outs[slot][:, pl.ds(place, size)] = part.astype(outs[slot].dtype)

        first[1].wait()
        put(
            columns - heads,
            heads,
            lax.dot_general(
                rows_in,
                step_in[...],
                (((1,), (1,)), ((), ())),
                preferred_element_type=jnp.float32,
            ),
        )
        total = None
        for copy, (index, start, size, left, wide_by) in zip(copies, pieces):
            copy.wait()
            product = jnp.dot(
                rows_in[:, start : start + size],
                weights_in[index][pl.ds(start, size), pl.ds(left, wide_by)],
                preferred_element_type=jnp.float32,
            )
            total = product if start == 0 else total + product
            if start + size == depth:
                put(bases[index] + left, wide_by, total)

    return local_kernel(
        body,
        "project",
        sent_narrow((block, columns), owners),
        [(tokens, IN_HBM), (step_weights, IN_HBM)] + [(w, IN_HBM) for w in weights],
        [
            pltpu.VMEM(tokens.shape, jnp.bfloat16),
            pltpu.VMEM(step_weights.shape, jnp.bfloat16),
            pltpu.VMEM(tokens.shape, jnp.float32),
            pltpu.VMEM((owners * block, depth), jnp.float32),
            pltpu.SemaphoreType.DMA((2 + len(pieces),)),
        ]
        + [pltpu.VMEM(w.shape, jnp.bfloat16) for w in weights],
        bytes_accessed=10 << 20,
    )


def split_in(values, terms):
    parts = []
    for _ in range(terms):
        part = values.astype(jnp.bfloat16)
        parts.append(part)
        values = values - part.astype(jnp.float32)
    return parts


def stacked(*parts):
    rows = sum(part.shape[0] for part in parts)
    parts = [part.astype(jnp.float32) for part in parts]
    parts.append(jnp.zeros((-rows % 8, parts[0].shape[1]), jnp.float32))
    return jnp.concatenate(parts, axis=0).astype(jnp.bfloat16)


def prepare(step_bias, decay_log, skip_gain, inner, arrays, weights, rows_first):
    heads = step_bias.shape[1]
    head_dim = inner // heads
    count = 4 + len(arrays)
    wanted = [shaped(a.shape, a.dtype) for a in arrays]
    wanted.append(shaped((rows_first, weights.shape[1]), weights.dtype))

    def body(*refs):
        sources, (params_ref, spread_ref), outs = refs[:count], refs[count : count + 2], refs[count + 2 :]
        loaded, sems = outs[:-2], outs[-1]
        rows_ref = outs[-2]
        sources = [*sources[:-1], sources[-1].at[pl.ds(0, rows_first)]]
        targets = [rows_ref.at[pl.ds(i, 1)] for i in range(3)] + list(loaded)
        copies = [
            pltpu.make_async_copy(source, target, sems.at[i])
            for i, (source, target) in enumerate(zip(sources, targets))
        ]
        for copy in copies:
            copy.start()
        head = lax.broadcasted_iota(jnp.int32, (heads, inner), 0) * head_dim
        channel = lax.broadcasted_iota(jnp.int32, (heads, inner), 1)
        inside = (channel >= head) & (channel < head + head_dim)
        spread = jnp.where(inside, 1.0, 0.0).astype(jnp.bfloat16)
        spread_ref[...] = spread
        for copy in copies[:3]:
            copy.wait()
        rows = rows_ref[...]
        rows = jnp.concatenate([rows[0:1], jnp.exp(rows[1:2]), rows[2:3]], axis=0)
        total = jnp.zeros((3, inner), jnp.float32)
        for part in reversed(split_in(rows, 3)):
            total += jnp.dot(part, spread, preferred_element_type=jnp.float32)
        params_ref[...] = total
        for copy in copies[3:]:
            copy.wait()

    params, spread, *loaded = local_kernel(
        body,
        "prepare",
        [shaped((3, inner)), shaped((heads, inner), jnp.bfloat16)]
        + wanted,
        [(a, IN_HBM) for a in (step_bias, decay_log, skip_gain, *arrays, weights)],
        [pltpu.VMEM((3, heads), jnp.float32), pltpu.SemaphoreType.DMA((count,))],
        bytes_accessed=4 << 20,
    )
    return params, spread, loaded


def mix(parts, head_params, spread, convs, windows, norm_gain, ssm_state, steps):
    own_rows, heads, head_dim, state_size = ssm_state.shape
    block, columns = parts[0].shape
    inner, width = convs[0].shape[1], convs[1].shape[1]
    groups = width // state_size
    heads_group = heads // groups
    channels = heads_group * head_dim
    taps = convs[0].shape[0]
    count = len(parts)
    edges = (0, inner, 2 * inner, 2 * inner + width, 2 * inner + 2 * width, columns)
    terms = 1 + steps

    def body(*refs):
        part_refs = refs[:count]
        params_ref, spread_ref, *rest = refs[count:]
        conv_refs, window_refs = rest[:3], rest[3:6]
        gain_ref, state_ref, normed_ref, pre_ref, coef_ref, write_ref = rest[6:]
        total = part_refs[0][...]
        for ref in part_refs[1:]:
            total = total + ref[...].astype(jnp.float32)
        rounded = total.astype(jnp.bfloat16).astype(jnp.float32)
        pre_ref[...] = rounded[:, edges[1] : edges[4]]
        gate, *newest = [rounded[:, edges[i] : edges[i + 1]] for i in range(4)]
        bias, rate, skip = [params_ref[i : i + 1] for i in range(3)]
        step_pre = jnp.dot(
            rounded[:, edges[4] :].astype(jnp.bfloat16),
            spread_ref[...],
            preferred_element_type=jnp.float32,
        )
        step_size = jax.nn.softplus(step_pre + bias)
        decay = jnp.exp(-step_size * rate)
        gate = silu_float(gate)
        normed = []
        for own in range(own_rows):
            mine = slice(own * steps, (own + 1) * steps)
            acts = []
            for which in range(3):
                taps_in = conv_refs[which][...]
                earlier = window_refs[which][own].astype(jnp.float32)
                line = jnp.concatenate([earlier, newest[which][mine]], axis=0)
                acts.append(
                    silu_float(
                        added([line[k : k + steps] * taps_in[k : k + 1] for k in range(taps)])
                    )
                )
            input_act, write_act, read_act = acts
            write_ref[pl.ds(own * steps, steps), :] = write_act
            decays = decay[mine]
            fresh = step_size[mine] * input_act
            coefs = [fresh[s : s + 1] for s in range(steps)]
            kept = jnp.ones_like(decays[0:1])
            for s in reversed(range(steps)):
                coefs[s] = coefs[s] * kept
                kept = kept * decays[s : s + 1]
            coef_ref[own] = jnp.concatenate([kept] + coefs, axis=0)
            normed.append([])
            for g in range(groups):
                span = slice(g * channels, (g + 1) * channels)
                lanes = slice(g * state_size, (g + 1) * state_size)
                state = state_ref[own, g * heads_group : (g + 1) * heads_group]
                state = state.reshape(channels, state_size)
                high, low = [p.astype(jnp.float32) for p in split_in(read_act[:, lanes], 2)]
                reads = jnp.concatenate([high, low], axis=0).astype(jnp.bfloat16)
                by_high, by_low = [
                    lax.dot_general(
                        reads, p, (((1,), (1,)), ((), ())), preferred_element_type=jnp.float32
                    )
                    for p in split_in(state, 2)
                ]
                product = by_high[:steps] + by_high[steps:] + by_low[:steps]
                values = []
                for s in range(steps):
                    value = product[s : s + 1]
                    for j in range(s + 1):
                        overlap = jnp.sum(
                            write_act[j : j + 1, lanes] * read_act[s : s + 1, lanes],
                            axis=1,
                            keepdims=True,
                        )
                        value = decays[j : j + 1, span] * value + fresh[j : j + 1, span] * overlap
                    values.append(value)
                value = jnp.concatenate(values, axis=0) + skip[:, span] * input_act[:, span]
                value = value * gate[mine, span]
                mean = jnp.mean(value * value, axis=1, keepdims=True)
                normed[own].append(value * lax.rsqrt(mean + 1e-05) * gain_ref[:, span])
        normed = [jnp.concatenate(row, axis=1) for row in normed]
        normed_ref[...] = jnp.concatenate(normed, axis=0).astype(jnp.bfloat16)

    return local_kernel(
        body,
        "mix",
        [
            shaped((block, inner), jnp.bfloat16),
            shaped((block, inner + 2 * width)),
            shaped((own_rows, terms, inner)),
            shaped((block, width)),
        ],
        [(a, IN_VMEM) for a in (*parts, head_params, spread, *convs, *windows, norm_gain, ssm_state)],
        bytes_accessed=4 << 20,
    )


def renew(pre, coefs, writes, windows, ssm_state, tokens):
    steps, rows_all, depth = tokens.shape
    own_rows, heads, head_dim, state_size = ssm_state.shape
    groups = writes.shape[1] // state_size
    heads_group = heads // groups
    inner = coefs.shape[2]
    widths = [w.shape[2] for w in windows]

    def body(pre_ref, coef_ref, write_ref, *rest):
        window_refs, (state_ref, tokens_ref, final_ref, current_ref) = rest[:3], rest[3:7]
        out_refs = rest[7:]
        for s in range(steps):
            current_ref[pl.ds(s * rows_all, rows_all), :] = tokens_ref[s].astype(jnp.float32)
        for own in range(own_rows):
            first = own * steps
            base = 0
            for window_ref, out_ref, width in zip(window_refs, out_refs, widths):
                line = jnp.concatenate(
                    [
                        window_ref[own].astype(jnp.float32),
                        pre_ref[pl.ds(first, steps), pl.ds(base, width)],
                    ],
                    axis=0,
                )
                out_ref[own] = line[steps:].astype(jnp.bfloat16)
                base += width
            coefs_high, coefs_low = split_in(coef_ref[own, 1 : 1 + steps, :], 2)
            writes_high, writes_low = split_in(write_ref[pl.ds(first, steps), :], 2)
            left = stacked(coefs_high, coefs_high, coefs_low)
            right = stacked(writes_high, writes_low, writes_high)
            for g in range(groups):
                fresh = lax.dot_general(
                    left[:, g * heads_group * head_dim : (g + 1) * heads_group * head_dim],
                    right[:, g * state_size : (g + 1) * state_size],
                    (((0,), (0,)), ((), ())),
                    preferred_element_type=jnp.float32,
                )
                for i in range(heads_group):
                    h = g * heads_group + i
                    kept = coef_ref[own, 0:1, pl.ds(h * head_dim, 1)]
                    final_ref[own, h] = (
                        kept * state_ref[own, h] + fresh[i * head_dim : (i + 1) * head_dim]
                    )

    return local_kernel(
        body,
        "renew",
        [shaped(ssm_state.shape), shaped((steps * rows_all, depth))]
        + [shaped(w.shape, jnp.bfloat16) for w in windows],
        [(a, IN_VMEM) for a in (pre, coefs, writes, *windows, ssm_state, tokens)],
        bytes_accessed=4 << 20,
    )


def fetch(array, start, after):
    rows = array.shape[0] - start

    def body(source, _, target, sem):
        copy = pltpu.make_async_copy(source.at[pl.ds(start, rows)], target, sem)
        copy.start()
        copy.wait()

    return local_kernel(
        body,
        "fetch",
        shaped((rows, array.shape[1]), array.dtype),
        [(array, IN_HBM), (after, IN_VMEM)],
        [pltpu.SemaphoreType.DMA],
        bytes_accessed=8 << 20,
    )


def project_out(normed, parts, steps):
    owners = len(normed)
    block, inner = normed[0].shape
    own_rows = block // steps
    rows = own_rows * owners

    def body(*refs):
        out_ref, sent_ref, lhs = refs[owners + len(parts) :]
        for slot in range(owners):
            owner = owner_of(slot, "expert")
            values = refs[slot][...].astype(jnp.float32)
            for own in range(own_rows):
                for s in range(steps):
                    row = s * rows + owner * own_rows + own
                    lhs[pl.ds(row, 1), :] = values[own * steps + s : own * steps + s + 1]
        products = []
        base = 0
        for ref in refs[owners : owners + len(parts)]:
            values = lhs[:, pl.ds(base, ref.shape[0])].astype(jnp.bfloat16)
            products.append(jnp.dot(values, ref[...], preferred_element_type=jnp.float32))
            base += ref.shape[0]
        total = added(products)
        out_ref[...] = total
        sent_ref[...] = total.astype(jnp.bfloat16)

    return local_kernel(
        body,
        "project_out",
        sent_narrow((rows * steps, parts[0].shape[1]), 2),
        [(a, IN_VMEM) for a in (*normed, *parts)],
        [pltpu.VMEM((rows * steps, inner), jnp.float32)],
        bytes_accessed=4 << 20,
    )


def slot_rows(slot, width):
    start = owner_of(slot, "expert") * width
    return pl.ds(pl.multiple_of(start, width) if pairwise("expert") else start, width)


def expert_near(moe_in, expert_up):
    count = len(moe_in)
    many, width = moe_in[0].shape
    local_experts, _, hidden_width = expert_up.shape

    def body(*refs):
        up_ref, out_ref = refs[count:]
        for e in range(local_experts):
            out_ref[e] = added(
                [
                    jnp.dot(
                        refs[slot][...],
                        up_ref[e, slot_rows(slot, width), :],
                        preferred_element_type=jnp.float32,
                    )
                    for slot in range(count)
                ]
            )

    return local_kernel(
        body,
        "expert_near",
        shaped((local_experts, many, hidden_width)),
        [(a, IN_VMEM) for a in (*moe_in, expert_up)],
        bytes_accessed=4 << 20,
    )


def row_weights(chosen_ref, gates_ref, local_experts):
    first = lax.axis_index("expert") * local_experts
    steps = chosen_ref.shape[0]
    return [
        jnp.concatenate(
            [
                jnp.sum(
                    jnp.where(chosen_ref[s] == first + e, gates_ref[s], 0.0),
                    axis=1,
                    keepdims=True,
                )
                for s in range(steps)
            ],
            axis=0,
        )
        for e in range(local_experts)
    ]


def gated_sum(hidden_ref, weights, down_ref, columns):
    return added(
        [
            weights[e]
            * jnp.dot(
                hidden_ref[e], down_ref[e, :, columns], preferred_element_type=jnp.float32
            )
            for e in range(len(weights))
        ]
    )


def experts_far(near, moe_in, chosen, gates, expert_up, expert_down, owners):
    count = len(moe_in)
    many, width = moe_in[0].shape
    local_experts, _, hidden_width = expert_up.shape
    far = range(1, owners)

    def body(*refs):
        near_ref, chosen_ref, gates_ref, up_ref, down_ref, hidden_ref, *outs = refs[count:]
        for e in range(local_experts):
            total = near_ref[e]
            for i in range(count):
                total += jnp.dot(
                    refs[i][...],
                    up_ref[e, slot_rows(owners - count + i, width), :],
                    preferred_element_type=jnp.float32,
                )
            total = jnp.maximum(total, 0.0)
            hidden_ref[e] = (total * total).astype(jnp.bfloat16)
        weights = row_weights(chosen_ref, gates_ref, local_experts)
        for slot, out in zip(far, outs):
            total = gated_sum(hidden_ref, weights, down_ref, slot_rows(slot, width))
            out[...] = total.astype(out.dtype)

    hidden, *outs = local_kernel(
        body,
        "experts_far",
        [shaped((local_experts, many, hidden_width), jnp.bfloat16)]
        + sent_narrow((many, width), 1 + len(far))[1:],
        [(a, IN_VMEM) for a in (*moe_in, near, chosen, gates, expert_up, expert_down)],
        bytes_accessed=16 << 20,
    )
    return hidden, outs


def experts_close(hidden, chosen, gates, expert_down, owners):
    local_experts, many, _ = hidden.shape
    width = expert_down.shape[2] // owners

    def body(hidden_ref, chosen_ref, gates_ref, down_ref, *outs):
        weights = row_weights(chosen_ref, gates_ref, local_experts)
        for slot, out in enumerate(outs):
            total = gated_sum(hidden_ref, weights, down_ref, slot_rows(slot, width))
            out[...] = total.astype(out.dtype)

    return local_kernel(
        body,
        "experts_close",
        sent_narrow((many, width), 1),
        [(a, IN_VMEM) for a in (hidden, chosen, gates, expert_down)],
        bytes_accessed=4 << 20,
    )


def finish(parts, shape):
    steps, rows, _ = shape

    def body(*refs):
        total = added([ref[...] for ref in refs[:-1]])
        for s in range(steps):
            refs[-1][s] = total[s * rows : (s + 1) * rows].astype(jnp.bfloat16)

    return local_kernel(body, "finish", shaped(shape, jnp.bfloat16), [(p, IN_VMEM) for p in parts])


def per_device(
    tokens,
    proj_gate,
    proj_input,
    proj_write,
    proj_read,
    proj_step,
    conv_input,
    conv_write,
    conv_read,
    window_input,
    window_write,
    window_read,
    step_bias,
    decay_log,
    skip_gain,
    norm_gain,
    ssm_state,
    out_proj,
    expert_up,
    expert_down,
    expert_ids,
    route_gates,
):
    steps = tokens.shape[0]
    inner = conv_input.shape[1]
    windows = (window_input, window_write, window_read)
    projected = project(
        lax.axis_size("expert"),
        tokens,
        (proj_gate, proj_input, proj_write, proj_read),
        proj_step.T,
    )
    head_params, spread, loaded = prepare(
        *[p.reshape(1, -1) for p in (step_bias, decay_log, skip_gain)],
        inner,
        (conv_input, conv_write, conv_read, *windows, norm_gain.reshape(1, -1), ssm_state)
        + (tokens, expert_ids, route_gates),
        out_proj,
        inner // FIRST,
    )
    convs, windows = loaded[:3], loaded[3:6]
    norm_gain, ssm_state, tokens, expert_ids, route_gates, out_first = loaded[6:]
    normed, pre, coefs, writes = mix(
        scatter_parts(projected, "expert"),
        head_params,
        spread,
        convs,
        windows,
        norm_gain,
        ssm_state,
        steps,
    )
    partial, sent = project_out(gather(normed, "expert"), (out_first, fetch(out_proj, inner // FIRST, writes)), steps)
    ssm_final, current, *finals = renew(pre, coefs, writes, windows, ssm_state, tokens)
    residual = added([current] + sum_parts(partial, "tensor", sent, ((2, 0, 3, 1), (3, 2, 1, 0), (1, 3, 0, 2))))
    moe_in = gather(residual.astype(jnp.bfloat16), "expert")
    expert_up, expert_down = resident(expert_up), resident(expert_down)
    near = expert_near(moe_in[:NEAR], expert_up)
    owners = len(moe_in)
    hidden, far = experts_far(
        near, moe_in[NEAR:], expert_ids, route_gates, expert_up, expert_down, owners
    )
    moe_sum = [*experts_close(hidden, expert_ids, route_gates, expert_down, owners), *far]
    moe_sum = added(scatter_parts(moe_sum, "expert"))
    mixed_out = finish([residual] + sum_parts(moe_sum, "tensor", moe_sum.astype(jnp.bfloat16), ((1, 0, 3, 2), (2, 3, 0, 1), (3, 2, 1, 0))), tokens.shape)
    return (mixed_out, ssm_final, *finals)


def solution(mesh):
    placed = (
        P(None, "groups", "expert"),
        P("expert", "tensor"),
        P("expert", "tensor"),
        P("expert", "tensor"),
        P("expert", "tensor"),
        P("expert", "tensor"),
        P(None, "tensor"),
        P(None, "tensor"),
        P(None, "tensor"),
        P(("groups", "expert"), None, "tensor"),
        P(("groups", "expert"), None, "tensor"),
        P(("groups", "expert"), None, "tensor"),
        P("tensor"),
        P("tensor"),
        P("tensor"),
        P("tensor"),
        P(("groups", "expert"), "tensor", None, None),
        P("tensor", "expert"),
        P("expert", None, "tensor"),
        P("expert", "tensor", None),
        P(None, "groups", None),
        P(None, "groups", None),
    )
    return jax.shard_map(
        per_device,
        mesh=mesh,
        in_specs=placed,
        out_specs=(
            P(None, "groups", "expert"),
            P(("groups", "expert"), "tensor", None, None),
            P(("groups", "expert"), None, "tensor"),
            P(("groups", "expert"), None, "tensor"),
            P(("groups", "expert"), None, "tensor"),
        ),
        check_vma=False,
    )
```
